256 devices in a mesh: gy: 16 (over y_lo, z), gx: 8 (over x, core), gz: 2 (over y_hi).
Axes of the slice: x: 4, y: 4 (y_hi: 2, y_lo: 2; y = y_hi * 2 + y_lo), z: 8, core: 2. Of those that a mesh axis runs over, the one named last changes fastest.
Arguments:
- fields: float32 [4, 128, 256, 256], P(None, 'gx', 'gy', 'gz'), may hold values from -0.3 to 0.3
- previous: float32 [3, 128, 256, 256], P(None, 'gx', 'gy', 'gz'), may hold values from -0.3 to 0.3
- cotangent: float32 [4, 128, 256, 256], P(None, 'gx', 'gy', 'gz'), may hold values from -0.3 to 0.3
Outputs:
- residual: float32 [4, 128, 256, 256], P(None, 'gx', 'gy', 'gz')
- adjoint: float32 [4, 128, 256, 256], P(None, 'gx', 'gy', 'gz')
The draws below stay inside these ranges and needn't reach their ends.
All inputs are finite; a program needn't handle non-finite values.
Results may differ from the reference program's by a relative error of at most 0.000096.
Values sent between devices are 32-bit elements; how exact they have to be, the bound alone decides.
No kernel may reach another device: no remote copies, remote signals or barrier semaphores. Data moves between devices by JAX's collectives and lax.ppermute only.
A program may use at most 128 MiB of HBM per device.

```python
import math
import jax
import jax.numpy as jnp
from jax import lax

NY = 256
NX = 128
NZ = 256


def wave_lines(key, count, low_period, high_period):
    rows = jnp.arange(NY, dtype=jnp.int32)
    flip = jnp.where(rows % 2 == 0, 1.0, -1.0).astype(jnp.float32)
    grid = rows.astype(jnp.float32)[None, None, :, None]
    summed = jnp.zeros((count, NX, NY, NZ), jnp.float32)
    for term in range(3):
        term_key = jax.random.fold_in(key, term + 1)
        key_freq, key_phase, key_amp = jax.random.split(term_key, 3)
        freq = jax.random.uniform(key_freq, (count, NX, 1, NZ), jnp.float32, 2.0 * math.pi / high_period, 2.0 * math.pi / low_period)
        phase = jax.random.uniform(key_phase, (count, NX, 1, NZ), jnp.float32, -math.pi, math.pi)
        amp = jax.random.uniform(key_amp, (count, NX, 1, NZ), jnp.float32, -1.0, 1.0)
        summed = summed + amp * jnp.cos(freq * grid + phase)
    return flip[None, None, :, None] * summed


def draw_fields(key, part):
    key = jax.random.fold_in(key, 11)
    key_noise, key_wave = jax.random.split(key)
    waves = wave_lines(key_wave, 4, 8.0, 24.0)
    noise = jax.random.normal(key_noise, (4, NX, NY, NZ), jnp.float32)
    mixed = 0.05 * (0.5 * noise + 0.8 * waves)
    return jnp.clip(mixed, -0.3, 0.3)


def draw_cotangent(key, part):
    key = jax.random.fold_in(key, 12)
    key_noise, key_wave = jax.random.split(key)
    waves = wave_lines(key_wave, 4, 8.0, 24.0)
    noise = jax.random.normal(key_noise, (4, NX, NY, NZ), jnp.float32)
    mixed = 0.05 * (0.5 * noise + 0.8 * waves)
    return jnp.clip(mixed, -0.3, 0.3)


def block_levels(stream_key, dims, shards, smallest, top_value):
    def one(position, shards_of):
        steps = jax.random.uniform(jax.random.fold_in(jax.random.fold_in(stream_key, 6), position), (shards_of,), jnp.float32, smallest / len(shards), top_value / len(shards))
        return jnp.repeat(jnp.exp(steps), dims[position] // shards_of).reshape((-1,) + (1,) * (len(dims) - position - 1))

    loudness = one(*shards[0])
    for cut in shards[1:]:
        loudness = loudness * one(*cut)
    return loudness


def normal_values(rng, dims, deviation, most, shards=(), kind=jnp.bfloat16):
    values = deviation * jax.random.normal(rng, dims, jnp.float32)
    if shards:
        values = values * block_levels(rng, dims, shards, -0.22, 0.18)
    return jnp.clip(values, -most, most).astype(kind)


def setup_inputs(seed: int = 0) -> dict:
    streams_of = jax.random.split(jax.random.key(seed), 4)
    return {
        "fields": draw_fields(jax.random.fold_in(streams_of[3], 71), 0),
        "previous": normal_values(streams_of[1], (3, NX, NY, NZ), 0.05, 0.3, ((1, 8), (2, 16), (3, 2)), jnp.float32),
        "cotangent": draw_cotangent(jax.random.fold_in(streams_of[3], 71), 0),
    }


NU_VALUE = 0.001
STEP_DT = 0.1
SPACE_X = 8.0 * math.pi / 512.0
SPACE_Z = 3.0 * math.pi / 512.0
first_coeffs = (0.8, -0.2, 4.0 / 105.0, -1.0 / 280.0)
second_coeffs = (1.6, -0.2, 8.0 / 315.0, -1.0 / 560.0)
center_coeff = -205.0 / 72.0

def chebyshev_pair(points):
    final_row = points - 1
    positions = jnp.arange(points, dtype=jnp.int32)
    row_ids = positions[:, None].astype(jnp.float32)
    col_ids = positions[None, :].astype(jnp.float32)
    half_step = math.pi / (2.0 * final_row)
    spacing = -2.0 * jnp.sin(half_step * (row_ids + col_ids)) * jnp.sin(half_step * (row_ids - col_ids))
    ends = jnp.where((positions == 0) | (positions == final_row), 2.0, 1.0)
    signs = jnp.where(positions % 2 == 0, 1.0, -1.0)
    scaled = (ends * signs).astype(jnp.float32)
    diagonal = positions[:, None] == positions[None, :]
    entries = scaled[:, None] / scaled[None, :] / jnp.where(diagonal, 1.0, spacing)
    entries = jnp.where(diagonal, 0.0, entries)
    first_mat = entries - jnp.diag(lax.optimization_barrier(jnp.sum(entries, axis=1)))
    second_mat = jnp.dot(first_mat, first_mat, precision=lax.Precision.HIGHEST)
    return (first_mat, second_mat)

def wall_profile(positions, points):
    final_row = points - 1
    angles = positions.astype(jnp.float32) * (math.pi / final_row)
    weight = jnp.sin(angles) ** 4
    wall_rows = jnp.where((positions == 0) | (positions == final_row), 1.0, 0.0).astype(jnp.float32)
    return (weight, wall_rows)

def first_roll(field, axis, space):
    summed = jnp.zeros_like(field)
    for distance, factor in enumerate(first_coeffs):
        summed = summed + factor * (jnp.roll(field, -(distance + 1), axis) - jnp.roll(field, distance + 1, axis))
    return summed / space

def second_roll(field, axis, space):
    summed = center_coeff * field
    for distance, factor in enumerate(second_coeffs):
        summed = summed + factor * (jnp.roll(field, -(distance + 1), axis) + jnp.roll(field, distance + 1, axis))
    return summed / (space * space)

def along_wall(matrix, field):
    return jnp.einsum('ij,cxjz->cxiz', matrix, field, precision=lax.Precision.HIGHEST)

def residual_of(fields, previous, first_mat, second_mat, weight, wall_rows):
    velocity = fields[0:3]
    slope_x = first_roll(fields, 1, SPACE_X)
    slope_y = along_wall(first_mat, fields)
    slope_z = first_roll(fields, 3, SPACE_Z)
    curve = second_roll(velocity, 1, SPACE_X) + along_wall(second_mat, velocity) + second_roll(velocity, 3, SPACE_Z)
    pressure_grad = jnp.stack([slope_x[3], slope_y[3], slope_z[3]])
    transport = fields[0:1] * slope_x[0:3] + fields[1:2] * slope_y[0:3] + fields[2:3] * slope_z[0:3]
    momentum = (velocity - previous) / STEP_DT + transport + pressure_grad - NU_VALUE * curve
    weight_b = weight[None, None, :, None]
    wall_b = wall_rows[None, None, :, None]
    balance = weight_b * momentum + wall_b * velocity
    continuity = weight_b[0] * (slope_x[0] + slope_y[1] + slope_z[2])
    return jnp.concatenate([balance, continuity[None]], axis=0)

def reference(fields, previous, cotangent):
    points = fields.shape[2]
    first_mat, second_mat = chebyshev_pair(points)
    weight, wall_rows = wall_profile(jnp.arange(points, dtype=jnp.int32), points)

    def evaluate(values):
        return residual_of(values, previous, first_mat, second_mat, weight, wall_rows)
    residual, pullback = jax.vjp(evaluate, fields)
    adjoint = pullback(cotangent)[0]
    return (residual, adjoint)
```

```python
import functools
import math

import jax
import jax.numpy as jnp
import numpy as np
from jax import lax
from jax.experimental import pallas as pl
from jax.experimental.pallas import tpu as pltpu
from jax.sharding import PartitionSpec as P

NU_VALUE = 0.001
STEP_DT = 0.1
SPACE_X = 8.0 * math.pi / 512.0
SPACE_Z = 3.0 * math.pi / 512.0
first_coeffs = (0.8, -0.2, 4.0 / 105.0, -1.0 / 280.0)
second_coeffs = (1.6, -0.2, 8.0 / 315.0, -1.0 / 560.0)
center_coeff = -205.0 / 72.0
VMEM_BYTES = 48 * 1024 * 1024
EXACT = lax.Precision.HIGHEST
f32 = jnp.float32


def wall_matrices(points):
    final_row = points - 1
    j = np.arange(points)
    half = math.pi / (2.0 * final_row)
    spacing = -2.0 * np.sin(half * (j[:, None] + j[None, :])) * np.sin(half * (j[:, None] - j[None, :]))
    ends = np.where((j == 0) | (j == final_row), 2.0, 1.0) * np.where(j % 2 == 0, 1.0, -1.0)
    eye = np.eye(points, dtype=bool)
    entries = np.where(eye, 0.0, ends[:, None] / ends[None, :] / np.where(eye, 1.0, spacing))
    first = entries - np.diag(entries.sum(axis=1))
    second = first @ first
    return first.astype(np.float32), second.astype(np.float32)


def wall_profile(points):
    final_row = points - 1
    j = np.arange(points)
    weight = np.sin(j * (math.pi / final_row)) ** 4
    wall = np.where((j == 0) | (j == final_row), 1.0, 0.0)
    return (
        np.repeat(weight[:, None], 128, 1).astype(np.float32),
        np.repeat(wall[:, None], 128, 1).astype(np.float32),
    )


def call(kernel, outs, args, flops, scratch=()):
    moved = sum(4 * math.prod(a.shape) for a in (*outs, *args))
    return pl.pallas_call(
        kernel,
        out_shape=outs,
        scratch_shapes=list(scratch),
        cost_estimate=pl.CostEstimate(flops=flops, bytes_accessed=moved, transcendentals=0),
        compiler_params=pltpu.CompilerParams(vmem_limit_bytes=VMEM_BYTES),
    )(*args)


def like(*shape):
    return jax.ShapeDtypeStruct(shape, f32)


def swap_kernel(a_ref, out_ref):
    for c in range(a_ref.shape[0]):
        out_ref[:, c] = a_ref[c]


def faces_kernel(fields_ref, cot_ref, cot_out, last_out, lead_out, zed_out):
    comps, cells = cot_ref.shape[0:2]
    for c in range(comps):
        cot_out[:, c] = cot_ref[c]
        last_out[c] = fields_ref[c, cells - 4 : cells]
        last_out[comps + c] = cot_ref[c, cells - 4 : cells]
        lead_out[c] = fields_ref[c, 0:4]
        lead_out[comps + c] = cot_ref[c, 0:4]

    def plane(x, _):
        lane = lax.broadcasted_iota(jnp.int32, zed_out.shape[1:], 1)
        total = jnp.zeros(zed_out.shape[1:], f32)
        for c in range(2 * comps):
            value = fields_ref[c, x] if c < comps else cot_ref[c - comps, x]
            moved = pltpu.roll(value, 4 + 8 * c, 1)
            total = jnp.where((lane >= 8 * c) & (lane < 8 * c + 8), moved, total)
        zed_out[x] = total
        return 0

    lax.fori_loop(0, cells, plane, 0)


def stencils(values, space, need_first, need_second):
    first = second = None
    if need_first:
        for k in range(4):
            term = (first_coeffs[k] / space) * (values[5 + k] - values[3 - k])
            first = term if first is None else first + term
    if need_second:
        second = (center_coeff / (space * space)) * values[4]
        for k in range(4):
            second = second + (second_coeffs[k] / (space * space)) * (values[5 + k] + values[3 - k])
    return first, second


def local_kernel(
    fields_ref, prev_ref, cot_ref, before_ref, after_ref, zed_ref, weight_ref, wall_ref, at_ref,
    res_ref, adj_ref, ext,
):
    cells, rows, lanes = fields_ref.shape[1:]
    here = pl.ds(pl.multiple_of(at_ref[0] * rows, rows), rows)
    weight = weight_ref[here]
    wall = wall_ref[here]

    for c in range(4):
        ext[c, 0:4] = before_ref[c]
        ext[c, 4 : 4 + cells] = fields_ref[c]
        ext[c, 4 + cells :] = after_ref[c]
    for c in range(4):
        for x in range(cells + 8):
            if x < 4:
                value = before_ref[4 + c, x]
            elif x < 4 + cells:
                value = cot_ref[c, x - 4]
            else:
                value = after_ref[4 + c, x - 4 - cells]
            value = weight * value
            ext[4 + c, x] = value
            if c < 3:
                ext[8 + c, x] = ext[0, x] * value

    def plane(x, _):
        lane = lax.broadcasted_iota(jnp.int32, (rows, lanes), 1)
        packed = zed_ref[x]
        own = [ext[c, 4 + x] for c in range(8)]
        far = [pltpu.roll(packed, (lanes - 4 - 8 * c) % lanes, 1) for c in range(8)]
        for c in range(4, 8):
            far[c] = weight * far[c]
        for c in range(3):
            own.append(own[2] * own[4 + c])
            far.append(far[2] * far[4 + c])

        def along_x(c, need_first, need_second):
            return stencils([ext[c, x + k] for k in range(9)], SPACE_X, need_first, need_second)

        def along_z(c, need_first, need_second):
            values = [None] * 9
            values[4] = own[c]
            for k in range(1, 5):
                values[4 + k] = pltpu.roll(jnp.where(lane < k, far[c], own[c]), lanes - k, 1)
                values[4 - k] = pltpu.roll(jnp.where(lane >= lanes - k, far[c], own[c]), k, 1)
            return stencils(values, SPACE_Z, need_first, need_second)

        u = own[0:4]
        w = own[4:8]
        dx, dz, curve = [], [], []
        for c in range(4):
            fx, sx = along_x(c, True, c < 3)
            fz, sz = along_z(c, True, c < 3)
            dx.append(fx)
            dz.append(fz)
            curve.append(sx + sz if c < 3 else None)
        for c in range(3):
            moment = (u[c] - prev_ref[c, x]) * (1.0 / STEP_DT) + u[0] * dx[c] + u[2] * dz[c] - NU_VALUE * curve[c]
            if c == 0:
                moment = moment + dx[3]
            if c == 2:
                moment = moment + dz[3]
            res_ref[c, x] = weight * moment + wall * u[c]
        res_ref[3, x] = weight * (dx[0] + dz[2])

        wx = [along_x(4 + c, c in (0, 3), c < 3) for c in range(4)]
        wz = [along_z(4 + c, c in (2, 3), c < 3) for c in range(4)]
        for c in range(3):
            flux = along_x(8 + c, True, False)[0] + along_z(8 + c, True, False)[0]
            total = w[c] * (1.0 / STEP_DT) - flux - NU_VALUE * (wx[c][1] + wz[c][1]) + wall * cot_ref[c, x]
            if c == 0:
                total = total + (w[0] * dx[0] + w[1] * dx[1] + w[2] * dx[2]) - wx[3][0]
            if c == 2:
                total = total + (w[0] * dz[0] + w[1] * dz[1] + w[2] * dz[2]) - wz[3][0]
            adj_ref[c, x] = total
        adj_ref[3, x] = -(wx[0][0] + wz[2][0])
        return 0

    lax.fori_loop(0, cells, plane, 0)


def lines(ref, c):
    groups, _, rows, lanes = ref.shape
    return ref[:, c].reshape(groups * rows, lanes)


def blocks(value, groups):
    return value.reshape(groups, value.shape[0] // groups, value.shape[1])


def res_lines_kernel(first_ref, second_ref, weight_ref, f_ref, out_ref, slope_ref):
    groups = f_ref.shape[0]
    weight = weight_ref[...]
    u = [lines(f_ref, c) for c in range(4)]
    for c in range(3):
        slope = jnp.dot(first_ref[...], u[c], precision=EXACT, preferred_element_type=f32)
        curve = jnp.dot(second_ref[...], u[c], precision=EXACT, preferred_element_type=f32)
        slope_ref[c] = slope
        total = u[1] * slope - NU_VALUE * curve
        if c == 1:
            total = total + jnp.dot(first_ref[...], u[3], precision=EXACT, preferred_element_type=f32)
            out_ref[:, 3] = blocks(weight * slope, groups)
        out_ref[:, c] = blocks(weight * total, groups)


def adj_lines_kernel(first_t_ref, second_t_ref, weight_ref, f_ref, c_ref, slope_ref, out_ref):
    groups = f_ref.shape[0]
    weight = weight_ref[...]
    u2 = lines(f_ref, 1)
    w = [weight * lines(c_ref, c) for c in range(4)]
    for c in range(3):
        carried = u2 * w[c]
        if c == 1:
            carried = carried + w[3]
        total = jnp.dot(first_t_ref[...], carried, precision=EXACT, preferred_element_type=f32)
        total = total - NU_VALUE * jnp.dot(second_t_ref[...], w[c], precision=EXACT, preferred_element_type=f32)
        if c == 1:
            total = total + w[0] * slope_ref[0] + w[1] * slope_ref[1] + w[2] * slope_ref[2]
        out_ref[:, c] = blocks(total, groups)
    press = jnp.dot(first_t_ref[...], w[1], precision=EXACT, preferred_element_type=f32)
    out_ref[:, 3] = blocks(press, groups)


def add_kernel(a_ref, b_ref, out_ref):
    for c in range(a_ref.shape[0]):
        out_ref[c] = a_ref[c] + b_ref[:, c]


def per_device(fields, previous, cotangent):
    cells, rows, lanes = fields.shape[1:]
    groups = lax.axis_size("gy")
    points = rows * groups
    first, second = wall_matrices(points)
    weight, wall = wall_profile(points)
    at = lax.axis_index("gy").astype(jnp.int32).reshape(1)
    sent = like(cells, 4, rows, lanes)
    block = like(4, cells, rows, lanes)

    exchange = functools.partial(lax.all_to_all, axis_name="gy", split_axis=0, concat_axis=0, tiled=True)

    (f_out,) = call(swap_kernel, [sent], [fields], 0)
    f_lines = exchange(f_out)
    face = like(8, 4, rows, lanes)
    c_out, last, lead, zed = call(
        faces_kernel, [sent, face, face, like(cells, rows, lanes)], [fields, cotangent], 10**6
    )
    c_lines = exchange(c_out)

    gx = lax.axis_size("gx")
    gz = lax.axis_size("gz")
    before = lax.ppermute(last, "gx", [(i, (i + 1) % gx) for i in range(gx)])
    after = lax.ppermute(lead, "gx", [((i + 1) % gx, i) for i in range(gx)])
    zed = lax.ppermute(zed, "gz", [(i, (i + 1) % gz) for i in range(gz)])

    local_res, local_adj = pl.pallas_call(
        local_kernel,
        out_shape=[block, block],
        in_specs=[pl.BlockSpec(memory_space=pltpu.VMEM)] * 8 + [pl.BlockSpec(memory_space=pltpu.SMEM)],
        scratch_shapes=[pltpu.VMEM((11, cells + 8, rows, lanes), f32)],
        cost_estimate=pl.CostEstimate(flops=2 * 10**7, bytes_accessed=6 * 10**6, transcendentals=0),
        compiler_params=pltpu.CompilerParams(vmem_limit_bytes=VMEM_BYTES),
    )(fields, previous, cotangent, before, after, zed, jnp.asarray(weight), jnp.asarray(wall), at)

    wide = 2 * points * points * lanes * 42
    r_out, slope = call(
        res_lines_kernel,
        [like(groups, 4, rows, lanes), like(3, points, lanes)],
        [jnp.asarray(first), jnp.asarray(second), jnp.asarray(weight), f_lines],
        wide,
    )
    r_back = exchange(r_out)
    (a_out,) = call(
        adj_lines_kernel,
        [like(groups, 4, rows, lanes)],
        [
            jnp.asarray(np.ascontiguousarray(first.T)),
            jnp.asarray(np.ascontiguousarray(second.T)),
            jnp.asarray(weight),
            f_lines,
            c_lines,
            slope,
        ],
        wide,
    )
    a_back = exchange(a_out)
    (residual,) = call(add_kernel, [block], [local_res, r_back], 10**6)
    (adjoint,) = call(add_kernel, [block], [local_adj, a_back], 10**6)
    return residual, adjoint


def solution(mesh):
    spec = P(None, "gx", "gy", "gz")
    return jax.shard_map(
        per_device, mesh=mesh, in_specs=(spec,) * 3, out_specs=(spec,) * 2, check_vma=False
    )
```

```python
import functools
import math

import jax
import jax.numpy as jnp
import numpy as np
from jax import lax
from jax.experimental import pallas as pl
from jax.experimental.pallas import tpu as pltpu
from jax.sharding import PartitionSpec as P

NU_VALUE = 0.001
STEP_DT = 0.1
SPACE_X = 8.0 * math.pi / 512.0
SPACE_Z = 3.0 * math.pi / 512.0
first_coeffs = (0.8, -0.2, 4.0 / 105.0, -1.0 / 280.0)
second_coeffs = (1.6, -0.2, 8.0 / 315.0, -1.0 / 560.0)
center_coeff = -205.0 / 72.0
VMEM_BYTES = 48 * 1024 * 1024
EXACT = lax.Precision.HIGHEST
f32 = jnp.float32


def wall_matrices(points):
    final_row = points - 1
    j = np.arange(points)
    half = math.pi / (2.0 * final_row)
    spacing = -2.0 * np.sin(half * (j[:, None] + j[None, :])) * np.sin(half * (j[:, None] - j[None, :]))
    ends = np.where((j == 0) | (j == final_row), 2.0, 1.0) * np.where(j % 2 == 0, 1.0, -1.0)
    eye = np.eye(points, dtype=bool)
    entries = np.where(eye, 0.0, ends[:, None] / ends[None, :] / np.where(eye, 1.0, spacing))
    first = entries - np.diag(entries.sum(axis=1))
    second = first @ first
    return first.astype(np.float32), second.astype(np.float32)


def wall_profile(points):
    final_row = points - 1
    j = np.arange(points)
    weight = np.sin(j * (math.pi / final_row)) ** 4
    wall = np.where((j == 0) | (j == final_row), 1.0, 0.0)
    return (
        np.repeat(weight[:, None], 128, 1).astype(np.float32),
        np.repeat(wall[:, None], 128, 1).astype(np.float32),
    )


def call(kernel, outs, args, flops, scratch=()):
    moved = sum(4 * math.prod(a.shape) for a in (*outs, *args))
    return pl.pallas_call(
        kernel,
        out_shape=outs,
        scratch_shapes=list(scratch),
        cost_estimate=pl.CostEstimate(flops=flops, bytes_accessed=moved, transcendentals=0),
        compiler_params=pltpu.CompilerParams(vmem_limit_bytes=VMEM_BYTES),
    )(*args)


def like(*shape):
    return jax.ShapeDtypeStruct(shape, f32)


def pack_kernel(fields_ref, cot_ref, sent_out, last_out, lead_out):
    comps, cells = cot_ref.shape[0:2]
    for c in range(comps):
        for ref, slot in ((fields_ref, c), (cot_ref, comps + c)):
            sent_out[:, slot] = ref[c]
            last_out[slot] = ref[c, cells - 4 : cells]
            lead_out[slot] = ref[c, 0:4]


def zed_kernel(fields_ref, cot_ref, zed_out):
    comps, cells = cot_ref.shape[0:2]

    def plane(x, _):
        lane = lax.broadcasted_iota(jnp.int32, zed_out.shape[1:], 1)
        total = jnp.zeros(zed_out.shape[1:], f32)
        for c in range(2 * comps):
            value = fields_ref[c, x] if c < comps else cot_ref[c - comps, x]
            moved = pltpu.roll(value, 4 + 8 * c, 1)
            total = jnp.where((lane >= 8 * c) & (lane < 8 * c + 8), moved, total)
        zed_out[x] = total
        return 0

    lax.fori_loop(0, cells, plane, 0)


def stencils(values, space, need_first, need_second):
    first = second = None
    if need_first:
        for k in range(4):
            term = (first_coeffs[k] / space) * (values[5 + k] - values[3 - k])
            first = term if first is None else first + term
    if need_second:
        second = (center_coeff / (space * space)) * values[4]
        for k in range(4):
            second = second + (second_coeffs[k] / (space * space)) * (values[5 + k] + values[3 - k])
    return first, second


def local_kernel(
    fields_ref, prev_ref, cot_ref, before_ref, after_ref, zed_ref, weight_ref, wall_ref, at_ref,
    res_ref, adj_ref, ext,
):
    cells, rows, lanes = fields_ref.shape[1:]
    here = pl.ds(pl.multiple_of(at_ref[0] * rows, rows), rows)
    weight = weight_ref[here]
    wall = wall_ref[here]

    for c in range(4):
        ext[c, 0:4] = before_ref[c]
        ext[c, 4 : 4 + cells] = fields_ref[c]
        ext[c, 4 + cells :] = after_ref[c]
    for c in range(4):
        for x in range(cells + 8):
            if x < 4:
                value = before_ref[4 + c, x]
            elif x < 4 + cells:
                value = cot_ref[c, x - 4]
            else:
                value = after_ref[4 + c, x - 4 - cells]
            value = weight * value
            ext[4 + c, x] = value
            if c < 3:
                ext[8 + c, x] = ext[0, x] * value

    def plane(x, _):
        lane = lax.broadcasted_iota(jnp.int32, (rows, lanes), 1)
        packed = zed_ref[x]
        own = [ext[c, 4 + x] for c in range(8)]
        far = [pltpu.roll(packed, (lanes - 4 - 8 * c) % lanes, 1) for c in range(8)]
        for c in range(4, 8):
            far[c] = weight * far[c]
        for c in range(3):
            own.append(own[2] * own[4 + c])
            far.append(far[2] * far[4 + c])

        def along_x(c, need_first, need_second):
            return stencils([ext[c, x + k] for k in range(9)], SPACE_X, need_first, need_second)

        def along_z(c, need_first, need_second):
            values = [None] * 9
            values[4] = own[c]
            for k in range(1, 5):
                values[4 + k] = pltpu.roll(jnp.where(lane < k, far[c], own[c]), lanes - k, 1)
                values[4 - k] = pltpu.roll(jnp.where(lane >= lanes - k, far[c], own[c]), k, 1)
            return stencils(values, SPACE_Z, need_first, need_second)

        u = own[0:4]
        w = own[4:8]
        dx, dz, curve = [], [], []
        for c in range(4):
            fx, sx = along_x(c, True, c < 3)
            fz, sz = along_z(c, True, c < 3)
            dx.append(fx)
            dz.append(fz)
            curve.append(sx + sz if c < 3 else None)
        for c in range(3):
            moment = (u[c] - prev_ref[c, x]) * (1.0 / STEP_DT) + u[0] * dx[c] + u[2] * dz[c] - NU_VALUE * curve[c]
            if c == 0:
                moment = moment + dx[3]
            if c == 2:
                moment = moment + dz[3]
            res_ref[c, x] = weight * moment + wall * u[c]
        res_ref[3, x] = weight * (dx[0] + dz[2])

        wx = [along_x(4 + c, c in (0, 3), c < 3) for c in range(4)]
        wz = [along_z(4 + c, c in (2, 3), c < 3) for c in range(4)]
        for c in range(3):
            flux = along_x(8 + c, True, False)[0] + along_z(8 + c, True, False)[0]
            total = w[c] * (1.0 / STEP_DT) - flux - NU_VALUE * (wx[c][1] + wz[c][1]) + wall * cot_ref[c, x]
            if c == 0:
                total = total + (w[0] * dx[0] + w[1] * dx[1] + w[2] * dx[2]) - wx[3][0]
            if c == 2:
                total = total + (w[0] * dz[0] + w[1] * dz[1] + w[2] * dz[2]) - wz[3][0]
            adj_ref[c, x] = total
        adj_ref[3, x] = -(wx[0][0] + wz[2][0])
        return 0

    lax.fori_loop(0, cells, plane, 0)


def lines(ref, c):
    groups, _, rows, lanes = ref.shape
    return ref[:, c].reshape(groups * rows, lanes)


def blocks(value, groups):
    return value.reshape(groups, value.shape[0] // groups, value.shape[1])


def product(matrix_ref, values):
    lanes = values[0].shape[1]
    wide = jnp.dot(
        matrix_ref[...], jnp.concatenate(values, axis=1), precision=EXACT, preferred_element_type=f32
    )
    return [wide[:, i * lanes : (i + 1) * lanes] for i in range(len(values))]


def lines_kernel(first_ref, second_ref, first_t_ref, second_t_ref, weight_ref, in_ref, out_ref):
    groups = in_ref.shape[0]
    weight = weight_ref[...]
    u = [lines(in_ref, c) for c in range(4)]
    slope = product(first_ref, u)
    curve = product(second_ref, u[0:3])
    for c in range(3):
        total = u[1] * slope[c] - NU_VALUE * curve[c]
        if c == 1:
            total = total + slope[3]
        out_ref[:, c] = blocks(weight * total, groups)
    out_ref[:, 3] = blocks(weight * slope[1], groups)
    w = [weight * lines(in_ref, 4 + c) for c in range(4)]
    stretch = w[0] * slope[0] + w[1] * slope[1] + w[2] * slope[2]
    carried = [u[1] * w[0], u[1] * w[1] + w[3], u[1] * w[2], w[1]]
    lifted = product(first_t_ref, carried)
    bent = product(second_t_ref, w[0:3])
    for c in range(3):
        total = lifted[c] - NU_VALUE * bent[c]
        if c == 1:
            total = total + stretch
        out_ref[:, 4 + c] = blocks(total, groups)
    out_ref[:, 7] = blocks(lifted[3], groups)


def add_kernel(res_ref, adj_ref, back_ref, res_out, adj_out):
    for c in range(4):
        res_out[c] = res_ref[c] + back_ref[:, c]
        adj_out[c] = adj_ref[c] + back_ref[:, 4 + c]


def per_device(fields, previous, cotangent):
    cells, rows, lanes = fields.shape[1:]
    groups = lax.axis_size("gy")
    points = rows * groups
    first, second = wall_matrices(points)
    weight, wall = wall_profile(points)
    at = lax.axis_index("gy").astype(jnp.int32).reshape(1)
    sent = like(cells, 8, rows, lanes)
    face = like(8, 4, rows, lanes)
    block = like(4, cells, rows, lanes)
    gx, gz = lax.axis_size("gx"), lax.axis_size("gz")

    exchange = functools.partial(lax.all_to_all, axis_name="gy", split_axis=0, concat_axis=0, tiled=True)

    packed, last, lead = call(pack_kernel, [sent, face, face], [fields, cotangent], 0)
    gathered = exchange(packed)
    (zed,) = call(zed_kernel, [like(cells, rows, lanes)], [fields, cotangent], 10**6)
    before = lax.ppermute(last, "gx", [(i, (i + 1) % gx) for i in range(gx)])
    after = lax.ppermute(lead, "gx", [((i + 1) % gx, i) for i in range(gx)])
    zed = lax.ppermute(zed, "gz", [(i, (i + 1) % gz) for i in range(gz)])

    local_res, local_adj = pl.pallas_call(
        local_kernel,
        out_shape=[block, block],
        in_specs=[pl.BlockSpec(memory_space=pltpu.VMEM)] * 8 + [pl.BlockSpec(memory_space=pltpu.SMEM)],
        scratch_shapes=[pltpu.VMEM((11, cells + 8, rows, lanes), f32)],
        cost_estimate=pl.CostEstimate(flops=2 * 10**7, bytes_accessed=6 * 10**6, transcendentals=0),
        compiler_params=pltpu.CompilerParams(vmem_limit_bytes=VMEM_BYTES),
    )(fields, previous, cotangent, before, after, zed, jnp.asarray(weight), jnp.asarray(wall), at)

    matrices = [first, second, np.ascontiguousarray(first.T), np.ascontiguousarray(second.T), weight]
    (lined,) = call(
        lines_kernel,
        [like(groups, 8, rows, lanes)],
        [jnp.asarray(m) for m in matrices] + [gathered],
        2 * points * points * lanes * 14 * 6,
    )
    back = exchange(lined)
    residual, adjoint = call(add_kernel, [block, block], [local_res, local_adj, back], 10**6)
    return residual, adjoint


def solution(mesh):
    spec = P(None, "gx", "gy", "gz")
    return jax.shard_map(
        per_device, mesh=mesh, in_specs=(spec,) * 3, out_specs=(spec,) * 2, check_vma=False
    )
```

```python
import functools
import math

import jax
import jax.numpy as jnp
import numpy as np
from jax import lax
from jax.experimental import pallas as pl
from jax.experimental.pallas import tpu as pltpu
from jax.sharding import PartitionSpec as P

NU_VALUE = 0.001
STEP_DT = 0.1
SPACE_X = 8.0 * math.pi / 512.0
SPACE_Z = 3.0 * math.pi / 512.0
first_coeffs = (0.8, -0.2, 4.0 / 105.0, -1.0 / 280.0)
second_coeffs = (1.6, -0.2, 8.0 / 315.0, -1.0 / 560.0)
center_coeff = -205.0 / 72.0
VMEM_BYTES = 48 * 1024 * 1024
EXACT = lax.Precision.HIGHEST
f32 = jnp.float32


def wall_matrices(points):
    final_row = points - 1
    j = np.arange(points)
    half = math.pi / (2.0 * final_row)
    spacing = -2.0 * np.sin(half * (j[:, None] + j[None, :])) * np.sin(half * (j[:, None] - j[None, :]))
    ends = np.where((j == 0) | (j == final_row), 2.0, 1.0) * np.where(j % 2 == 0, 1.0, -1.0)
    eye = np.eye(points, dtype=bool)
    entries = np.where(eye, 0.0, ends[:, None] / ends[None, :] / np.where(eye, 1.0, spacing))
    first = entries - np.diag(entries.sum(axis=1))
    second = first @ first
    return first.astype(np.float32), second.astype(np.float32)


def wall_profile(points):
    final_row = points - 1
    j = np.arange(points)
    weight = np.sin(j * (math.pi / final_row)) ** 4
    wall = np.where((j == 0) | (j == final_row), 1.0, 0.0)
    return (
        np.repeat(weight[:, None], 128, 1).astype(np.float32),
        np.repeat(wall[:, None], 128, 1).astype(np.float32),
    )


def call(kernel, outs, args, flops, scratch=()):
    moved = sum(4 * math.prod(a.shape) for a in (*outs, *args))
    return pl.pallas_call(
        kernel,
        out_shape=outs,
        scratch_shapes=list(scratch),
        cost_estimate=pl.CostEstimate(flops=flops, bytes_accessed=moved, transcendentals=0),
        compiler_params=pltpu.CompilerParams(vmem_limit_bytes=VMEM_BYTES),
    )(*args)


def like(*shape):
    return jax.ShapeDtypeStruct(shape, f32)


def pack_kernel(fields_ref, cot_ref, sent_out, held, sems):
    comps = cot_ref.shape[0]
    copies = [
        pltpu.make_async_copy(fields_ref, held.at[0], sems.at[0]),
        pltpu.make_async_copy(cot_ref, held.at[1], sems.at[1]),
    ]
    for copy in copies:
        copy.start()
    for half, copy in enumerate(copies):
        copy.wait()
        for c in range(comps):
            sent_out[:, half * comps + c] = held[half, c]


def faces_kernel(fields_ref, cot_ref, last_out, lead_out, zed_out):
    comps, cells = cot_ref.shape[0:2]
    for c in range(comps):
        for ref, slot in ((fields_ref, c), (cot_ref, comps + c)):
            last_out[slot] = ref[c, cells - 4 : cells]
            lead_out[slot] = ref[c, 0:4]

    def plane(x, _):
        lane = lax.broadcasted_iota(jnp.int32, zed_out.shape[1:], 1)
        total = jnp.zeros(zed_out.shape[1:], f32)
        for c in range(2 * comps):
            value = fields_ref[c, x] if c < comps else cot_ref[c - comps, x]
            moved = pltpu.roll(value, 4 + 8 * c, 1)
            total = jnp.where((lane >= 8 * c) & (lane < 8 * c + 8), moved, total)
        zed_out[x] = total
        return 0

    lax.fori_loop(0, cells, plane, 0)


def stencils(values, space, need_first, need_second):
    first = second = None
    if need_first:
        for k in range(4):
            term = (first_coeffs[k] / space) * (values[5 + k] - values[3 - k])
            first = term if first is None else first + term
    if need_second:
        second = (center_coeff / (space * space)) * values[4]
        for k in range(4):
            second = second + (second_coeffs[k] / (space * space)) * (values[5 + k] + values[3 - k])
    return first, second


def local_kernel(
    fields_any, prev_any, cot_any, before_any, after_any, zed_any, weight_any, wall_any, at_ref,
    res_ref, adj_ref, ext, cot_ref, prev_ref, zed_ref, weight_ref, wall_ref, sems,
):
    cells, rows, lanes = fields_any.shape[1:]
    here = pl.ds(pl.multiple_of(at_ref[0] * rows, rows), rows)
    pairs = [
        (fields_any, ext.at[0:4, 4 : 4 + cells]),
        (before_any.at[0:4], ext.at[0:4, 0:4]),
        (after_any.at[0:4], ext.at[0:4, 4 + cells : 8 + cells]),
        (cot_any, cot_ref.at[:, 4 : 4 + cells]),
        (before_any.at[4:8], cot_ref.at[:, 0:4]),
        (after_any.at[4:8], cot_ref.at[:, 4 + cells : 8 + cells]),
        (prev_any, prev_ref),
        (zed_any, zed_ref),
        (weight_any.at[here], weight_ref),
        (wall_any.at[here], wall_ref),
    ]
    copies = [pltpu.make_async_copy(src, dst, sems.at[i]) for i, (src, dst) in enumerate(pairs)]
    for copy in copies:
        copy.start()
    for copy in copies:
        copy.wait()
    weight = weight_ref[...]
    wall = wall_ref[...]

    for c in range(4):
        for x in range(cells + 8):
            value = weight * cot_ref[c, x]
            ext[4 + c, x] = value
            if c < 3:
                ext[8 + c, x] = ext[0, x] * value

    def plane(x, _):
        lane = lax.broadcasted_iota(jnp.int32, (rows, lanes), 1)
        packed = zed_ref[x]
        own = [ext[c, 4 + x] for c in range(8)]
        far = [pltpu.roll(packed, (lanes - 4 - 8 * c) % lanes, 1) for c in range(8)]
        for c in range(4, 8):
            far[c] = weight * far[c]
        for c in range(3):
            own.append(own[2] * own[4 + c])
            far.append(far[2] * far[4 + c])

        def along_x(c, need_first, need_second):
            return stencils([ext[c, x + k] for k in range(9)], SPACE_X, need_first, need_second)

        def along_z(c, need_first, need_second):
            values = [None] * 9
            values[4] = own[c]
            for k in range(1, 5):
                values[4 + k] = pltpu.roll(jnp.where(lane < k, far[c], own[c]), lanes - k, 1)
                values[4 - k] = pltpu.roll(jnp.where(lane >= lanes - k, far[c], own[c]), k, 1)
            return stencils(values, SPACE_Z, need_first, need_second)

        u = own[0:4]
        w = own[4:8]
        dx, dz, curve = [], [], []
        for c in range(4):
            fx, sx = along_x(c, True, c < 3)
            fz, sz = along_z(c, True, c < 3)
            dx.append(fx)
            dz.append(fz)
            curve.append(sx + sz if c < 3 else None)
        for c in range(3):
            moment = (u[c] - prev_ref[c, x]) * (1.0 / STEP_DT) + u[0] * dx[c] + u[2] * dz[c] - NU_VALUE * curve[c]
            if c == 0:
                moment = moment + dx[3]
            if c == 2:
                moment = moment + dz[3]
            res_ref[c, x] = weight * moment + wall * u[c]
        res_ref[3, x] = weight * (dx[0] + dz[2])

        wx = [along_x(4 + c, c in (0, 3), c < 3) for c in range(4)]
        wz = [along_z(4 + c, c in (2, 3), c < 3) for c in range(4)]
        for c in range(3):
            flux = along_x(8 + c, True, False)[0] + along_z(8 + c, True, False)[0]
            total = w[c] * (1.0 / STEP_DT) - flux - NU_VALUE * (wx[c][1] + wz[c][1]) + wall * cot_ref[c, 4 + x]
            if c == 0:
                total = total + (w[0] * dx[0] + w[1] * dx[1] + w[2] * dx[2]) - wx[3][0]
            if c == 2:
                total = total + (w[0] * dz[0] + w[1] * dz[1] + w[2] * dz[2]) - wz[3][0]
            adj_ref[c, x] = total
        adj_ref[3, x] = -(wx[0][0] + wz[2][0])
        return 0

    lax.fori_loop(0, cells, plane, 0)


def lines(ref, c):
    groups, _, rows, lanes = ref.shape
    return ref[:, c].reshape(groups * rows, lanes)


def blocks(value, groups):
    return value.reshape(groups, value.shape[0] // groups, value.shape[1])


def product(matrix_ref, values):
    lanes = values[0].shape[1]
    wide = jnp.dot(
        matrix_ref[...], jnp.concatenate(values, axis=1), precision=EXACT, preferred_element_type=f32
    )
    return [wide[:, i * lanes : (i + 1) * lanes] for i in range(len(values))]


def lines_kernel(
    first_ref, second_ref, first_t_ref, second_t_ref, weight_ref, in_ref, out_ref, held, sems
):
    groups = in_ref.shape[0]
    weight = weight_ref[...]
    copies = []

    def send(slot, value):
        held[slot] = blocks(value, groups)
        copies.append(pltpu.make_async_copy(held.at[slot], out_ref.at[:, slot], sems.at[slot]))
        copies[-1].start()

    u = [lines(in_ref, c) for c in range(4)]
    w = [weight * lines(in_ref, 4 + c) for c in range(4)]
    slope = product(first_ref, u)
    curve = product(second_ref, u[0:3])
    for c in range(3):
        total = u[1] * slope[c] - NU_VALUE * curve[c]
        if c == 1:
            total = total + slope[3]
        send(c, weight * total)
    send(3, weight * slope[1])
    stretch = w[0] * slope[0] + w[1] * slope[1] + w[2] * slope[2]
    lifted = product(first_t_ref, [u[1] * w[0], u[1] * w[1] + w[3], u[1] * w[2], w[1]])
    send(7, lifted[3])
    bent = product(second_t_ref, w[0:3])
    for c in range(3):
        total = lifted[c] - NU_VALUE * bent[c]
        if c == 1:
            total = total + stretch
        send(4 + c, total)
    for copy in copies:
        copy.wait()


def add_kernel(res_ref, adj_ref, back_ref, res_out, adj_out):
    for c in range(4):
        res_out[c] = res_ref[c] + back_ref[:, c]
        adj_out[c] = adj_ref[c] + back_ref[:, 4 + c]


def per_device(fields, previous, cotangent):
    cells, rows, lanes = fields.shape[1:]
    groups = lax.axis_size("gy")
    points = rows * groups
    first, second = wall_matrices(points)
    weight, wall = wall_profile(points)
    at = lax.axis_index("gy").astype(jnp.int32).reshape(1)
    sent = like(cells, 8, rows, lanes)
    face = like(8, 4, rows, lanes)
    block = like(4, cells, rows, lanes)
    gx, gz = lax.axis_size("gx"), lax.axis_size("gz")

    exchange = functools.partial(lax.all_to_all, axis_name="gy", split_axis=0, concat_axis=0, tiled=True)

    packed = pl.pallas_call(
        pack_kernel,
        out_shape=pltpu.VMEM(sent.shape, f32),
        in_specs=[pl.BlockSpec(memory_space=pltpu.HBM)] * 2,
        out_specs=pl.BlockSpec(memory_space=pltpu.VMEM),
        scratch_shapes=[pltpu.VMEM((2,) + fields.shape, f32), pltpu.SemaphoreType.DMA((2,))],
    )(fields, cotangent)
    gathered = exchange(packed)
    last, lead, zed = call(
        faces_kernel, [face, face, like(cells, rows, lanes)], [fields, cotangent], 10**6
    )
    before = lax.ppermute(last, "gx", [(i, (i + 1) % gx) for i in range(gx)])
    after = lax.ppermute(lead, "gx", [((i + 1) % gx, i) for i in range(gx)])
    zed = lax.ppermute(zed, "gz", [(i, (i + 1) % gz) for i in range(gz)])

    far = pl.BlockSpec(memory_space=pltpu.HBM)
    local_res, local_adj = pl.pallas_call(
        local_kernel,
        out_shape=[pltpu.VMEM(block.shape, f32)] * 2,
        in_specs=[far] * 8 + [pl.BlockSpec(memory_space=pltpu.SMEM)],
        scratch_shapes=[
            pltpu.VMEM((11, cells + 8, rows, lanes), f32),
            pltpu.VMEM((4, cells + 8, rows, lanes), f32),
            pltpu.VMEM((3, cells, rows, lanes), f32),
            pltpu.VMEM((cells, rows, lanes), f32),
            pltpu.VMEM((rows, lanes), f32),
            pltpu.VMEM((rows, lanes), f32),
            pltpu.SemaphoreType.DMA((10,)),
        ],
        cost_estimate=pl.CostEstimate(flops=2 * 10**7, bytes_accessed=6 * 10**6, transcendentals=0),
    )(fields, previous, cotangent, before, after, zed, jnp.asarray(weight), jnp.asarray(wall), at)

    matrices = [first, second, np.ascontiguousarray(first.T), np.ascontiguousarray(second.T), weight]
    resident = pl.BlockSpec(memory_space=pltpu.VMEM)
    lined = pl.pallas_call(
        lines_kernel,
        out_shape=like(groups, 8, rows, lanes),
        in_specs=[resident] * 6,
        out_specs=pl.BlockSpec(memory_space=pltpu.HBM),
        scratch_shapes=[pltpu.VMEM((8, groups, rows, lanes), f32), pltpu.SemaphoreType.DMA((8,))],
        cost_estimate=pl.CostEstimate(
            flops=2 * points * points * lanes * 14 * 6, bytes_accessed=4 * 10**6, transcendentals=0
        ),
        compiler_params=pltpu.CompilerParams(vmem_limit_bytes=VMEM_BYTES),
    )(*[jnp.asarray(m) for m in matrices], gathered)
    back = exchange(lined)
    residual, adjoint = call(add_kernel, [block, block], [local_res, local_adj, back], 10**6)
    return residual, adjoint


def solution(mesh):
    spec = P(None, "gx", "gy", "gz")
    return jax.shard_map(
        per_device, mesh=mesh, in_specs=(spec,) * 3, out_specs=(spec,) * 2, check_vma=False
    )
```

```python
import functools
import math

import jax
import jax.numpy as jnp
import numpy as np
from jax import lax
from jax.experimental import pallas as pl
from jax.experimental.pallas import tpu as pltpu
from jax.sharding import PartitionSpec as P

NU_VALUE = 0.001
STEP_DT = 0.1
SPACE_X = 8.0 * math.pi / 512.0
SPACE_Z = 3.0 * math.pi / 512.0
first_coeffs = (0.8, -0.2, 4.0 / 105.0, -1.0 / 280.0)
second_coeffs = (1.6, -0.2, 8.0 / 315.0, -1.0 / 560.0)
center_coeff = -205.0 / 72.0
VMEM_BYTES = 48 * 1024 * 1024
WIDE_BYTES = 60 * 1024 * 1024
EXACT = lax.Precision.HIGHEST
f32 = jnp.float32


def wall_matrices(points):
    final_row = points - 1
    j = np.arange(points)
    half = math.pi / (2.0 * final_row)
    spacing = -2.0 * np.sin(half * (j[:, None] + j[None, :])) * np.sin(half * (j[:, None] - j[None, :]))
    ends = np.where((j == 0) | (j == final_row), 2.0, 1.0) * np.where(j % 2 == 0, 1.0, -1.0)
    eye = np.eye(points, dtype=bool)
    entries = np.where(eye, 0.0, ends[:, None] / ends[None, :] / np.where(eye, 1.0, spacing))
    first = entries - np.diag(entries.sum(axis=1))
    second = first @ first
    return first.astype(np.float32), second.astype(np.float32)


def wall_profile(points):
    final_row = points - 1
    j = np.arange(points)
    weight = np.sin(j * (math.pi / final_row)) ** 4
    return np.repeat(weight[:, None], 128, 1).astype(np.float32)


def call(kernel, outs, args, flops, scratch=()):
    moved = sum(4 * math.prod(a.shape) for a in (*outs, *args))
    return pl.pallas_call(
        kernel,
        out_shape=outs,
        scratch_shapes=list(scratch),
        cost_estimate=pl.CostEstimate(flops=flops, bytes_accessed=moved, transcendentals=0),
        compiler_params=pltpu.CompilerParams(vmem_limit_bytes=VMEM_BYTES),
    )(*args)


def like(*shape):
    return jax.ShapeDtypeStruct(shape, f32)


def row_profile(at_ref, points, shape):
    row = at_ref[0] * shape[0] + lax.broadcasted_iota(jnp.int32, shape, 0)
    weight = jnp.sin(row.astype(f32) * (math.pi / (points - 1))) ** 4
    wall = jnp.where((row == 0) | (row == points - 1), 1.0, 0.0).astype(f32)
    return weight, wall


def load(pairs, sems):
    copies = [pltpu.make_async_copy(src, dst, sems.at[i]) for i, (src, dst) in enumerate(pairs)]
    for copy in copies:
        copy.start()
    for copy in copies:
        copy.wait()


def faces_kernel(fields_any, cot_any, _res, last_out, lead_out, sems):
    cells = fields_any.shape[1]
    load(
        [
            (fields_any.at[:, cells - 4 : cells], last_out.at[0:4]),
            (cot_any.at[:, cells - 4 : cells], last_out.at[4:8]),
            (fields_any.at[:, 0:4], lead_out.at[0:4]),
            (cot_any.at[:, 0:4], lead_out.at[4:8]),
        ],
        sems,
    )


def pack_faces(held, zed_out):
    def plane(x, _):
        lane = lax.broadcasted_iota(jnp.int32, zed_out.shape[1:], 1)
        total = jnp.zeros(zed_out.shape[1:], f32)
        for c in range(8):
            moved = pltpu.roll(held[c, x], 4 + 8 * c, 1)
            total = jnp.where((lane >= 8 * c) & (lane < 8 * c + 8), moved, total)
        zed_out[x] = total
        return 0

    lax.fori_loop(0, zed_out.shape[0], plane, 0, unroll=4)


def pack_kernel(fields_any, cot_any, sent_out, zed_out, held, in_sems, out_sems):
    ins, outs = [], []
    for c in range(4):
        for ref, slot in ((fields_any, c), (cot_any, 4 + c)):
            ins.append(pltpu.make_async_copy(ref.at[c], held.at[slot], in_sems.at[slot]))
            outs.append(pltpu.make_async_copy(held.at[slot], sent_out.at[:, slot], out_sems.at[slot]))
    for copy in ins:
        copy.start()
    for arrived, leaving in zip(ins, outs):
        arrived.wait()
        leaving.start()

    pack_faces(held, zed_out)
    for copy in outs:
        copy.wait()


def stencils(values, space, need_first, need_second):
    first = second = None
    if need_first:
        for k in range(4):
            term = (first_coeffs[k] / space) * (values[5 + k] - values[3 - k])
            first = term if first is None else first + term
    if need_second:
        second = (center_coeff / (space * space)) * values[4]
        for k in range(4):
            second = second + (second_coeffs[k] / (space * space)) * (values[5 + k] + values[3 - k])
    return first, second


def along_z_work(
    core, points, core_ref, at_ref, fields_any, prev_any, cot_any, zed_ref,
    res_ref, adj_ref, field_ref, cot_ref, prev_ref, sems,
):
    cells, rows, lanes = fields_any.shape[1:]

    @pl.when(core_ref[0] % 2 == core)
    def _():
        load([(fields_any, field_ref), (cot_any, cot_ref), (prev_any, prev_ref)], sems)
        weight, wall = row_profile(at_ref, points, (rows, lanes))

        def plane(x, _):
            lane = lax.broadcasted_iota(jnp.int32, (rows, lanes), 1)
            packed = zed_ref[x]
            u = [field_ref[c, x] for c in range(4)]
            w = [weight * cot_ref[c, x] for c in range(4)]
            far = [pltpu.roll(packed, (lanes - 4 - 8 * c) % lanes, 1) for c in range(8)]
            far_u = far[0:4]
            far_w = [weight * value for value in far[4:8]]

            def along(own, other, need_first, need_second):
                values = [None] * 9
                values[4] = own
                for k in range(1, 5):
                    values[4 + k] = pltpu.roll(jnp.where(lane < k, other, own), lanes - k, 1)
                    values[4 - k] = pltpu.roll(jnp.where(lane >= lanes - k, other, own), k, 1)
                return stencils(values, SPACE_Z, need_first, need_second)

            du = [along(u[c], far_u[c], True, c < 3) for c in range(4)]
            for c in range(3):
                moment = (u[c] - prev_ref[c, x]) * (1.0 / STEP_DT) + u[2] * du[c][0] - NU_VALUE * du[c][1]
                if c == 2:
                    moment = moment + du[3][0]
                res_ref[c, x] = weight * moment + wall * u[c]
            res_ref[3, x] = weight * du[2][0]
            dw = [along(w[c], far_w[c], c >= 2, c < 3) for c in range(4)]
            for c in range(3):
                flux = along(u[2] * w[c], far_u[2] * far_w[c], True, False)[0]
                total = w[c] * (1.0 / STEP_DT) - flux - NU_VALUE * dw[c][1] + wall * cot_ref[c, x]
                if c == 2:
                    stretch = w[0] * du[0][0] + w[1] * du[1][0] + w[2] * du[2][0]
                    total = total + stretch - dw[3][0]
                adj_ref[c, x] = total
            adj_ref[3, x] = -dw[2][0]
            return 0

        lax.fori_loop(0, cells, plane, 0)


def early_z_kernel(
    points, core_ref, at_ref, fields_any, prev_any, cot_any, zed_ref, _packed, _zed,
    _same, res_ref, adj_ref, _same_zed, *scratch,
):
    along_z_work(
        1, points, core_ref, at_ref, fields_any, prev_any, cot_any, zed_ref, res_ref, adj_ref, *scratch
    )


def late_z_kernel(
    points, core_ref, at_ref, fields_any, prev_any, cot_any, zed_ref, _res, _adj,
    res_ref, adj_ref, *scratch,
):
    along_z_work(
        0, points, core_ref, at_ref, fields_any, prev_any, cot_any, zed_ref, res_ref, adj_ref, *scratch
    )


def along_x_kernel(
    points, at_ref, fields_any, cot_any, before_any, after_any, _res, _adj,
    res_ref, adj_ref, ext, cot_ref, sems,
):
    cells, rows, lanes = fields_any.shape[1:]
    load(
        [
            (fields_any, ext.at[0:4, 4 : 4 + cells]),
            (before_any.at[0:4], ext.at[0:4, 0:4]),
            (after_any.at[0:4], ext.at[0:4, 4 + cells : 8 + cells]),
            (cot_any, cot_ref.at[:, 4 : 4 + cells]),
            (before_any.at[4:8], cot_ref.at[:, 0:4]),
            (after_any.at[4:8], cot_ref.at[:, 4 + cells : 8 + cells]),
        ],
        sems,
    )
    weight = row_profile(at_ref, points, (rows, lanes))[0]

    for c in range(4):
        for x in range(cells + 8):
            value = weight * cot_ref[c, x]
            ext[4 + c, x] = value
            if c < 3:
                ext[8 + c, x] = ext[0, x] * value

    def plane(x, _):
        def along(c, need_first, need_second):
            return stencils([ext[c, x + k] for k in range(9)], SPACE_X, need_first, need_second)

        u = ext[0, 4 + x]
        w = [ext[4 + c, 4 + x] for c in range(3)]
        du = [along(c, True, c < 3) for c in range(4)]
        for c in range(3):
            moment = u * du[c][0] - NU_VALUE * du[c][1]
            if c == 0:
                moment = moment + du[3][0]
            res_ref[c, x] += weight * moment
        res_ref[3, x] += weight * du[0][0]
        dw = [along(4 + c, c in (0, 3), c < 3) for c in range(4)]
        for c in range(3):
            total = -along(8 + c, True, False)[0] - NU_VALUE * dw[c][1]
            if c == 0:
                total = total + (w[0] * du[0][0] + w[1] * du[1][0] + w[2] * du[2][0]) - dw[3][0]
            adj_ref[c, x] += total
        adj_ref[3, x] += -dw[0][0]
        return 0

    lax.fori_loop(0, cells, plane, 0)


def lines(ref, c):
    groups, _, rows, lanes = ref.shape
    return ref[:, c].reshape(groups * rows, lanes)


def blocks(value, groups):
    return value.reshape(groups, value.shape[0] // groups, value.shape[1])


def product(matrix_ref, values):
    lanes = values[0].shape[1]
    wide = jnp.dot(
        matrix_ref[...], jnp.concatenate(values, axis=1), precision=EXACT, preferred_element_type=f32
    )
    return [wide[:, i * lanes : (i + 1) * lanes] for i in range(len(values))]


def lines_kernel(
    first_ref, second_ref, first_t_ref, second_t_ref, weight_ref, in_ref, _res, out_ref, held, sems
):
    groups = in_ref.shape[0]
    weight = weight_ref[...]
    copies = []

    def send(slot, value):
        held[slot] = blocks(value, groups)
        copies.append(pltpu.make_async_copy(held.at[slot], out_ref.at[:, slot], sems.at[slot]))
        copies[-1].start()

    u = [lines(in_ref, c) for c in range(4)]
    w = [weight * lines(in_ref, 4 + c) for c in range(4)]
    slope = product(first_ref, u)
    curve = product(second_ref, u[0:3])
    for c in range(3):
        total = u[1] * slope[c] - NU_VALUE * curve[c]
        if c == 1:
            total = total + slope[3]
        send(c, weight * total)
    send(3, weight * slope[1])
    stretch = w[0] * slope[0] + w[1] * slope[1] + w[2] * slope[2]
    lifted = product(first_t_ref, [u[1] * w[0], u[1] * w[1] + w[3], u[1] * w[2], w[1]])
    send(7, lifted[3])
    bent = product(second_t_ref, w[0:3])
    for c in range(3):
        total = lifted[c] - NU_VALUE * bent[c]
        if c == 1:
            total = total + stretch
        send(4 + c, total)
    for copy in copies:
        copy.wait()


def add_kernel(res_ref, adj_ref, back_ref, res_out, adj_out):
    for c in range(4):
        res_out[c] = res_ref[c] + back_ref[:, c]
        adj_out[c] = adj_ref[c] + back_ref[:, 4 + c]


def per_device(fields, previous, cotangent):
    cells, rows, lanes = fields.shape[1:]
    groups = lax.axis_size("gy")
    points = rows * groups
    first, second = wall_matrices(points)
    weight = wall_profile(points)
    sent = (cells, 8, rows, lanes)
    gx, gz = lax.axis_size("gx"), lax.axis_size("gz")
    at = lax.axis_index("gy").astype(jnp.int32).reshape(1)
    core_at = lax.axis_index("gx").astype(jnp.int32).reshape(1)
    exchange = functools.partial(lax.all_to_all, axis_name="gy", split_axis=0, concat_axis=0, tiled=True)
    far = pl.BlockSpec(memory_space=pltpu.HBM)
    near = pl.BlockSpec(memory_space=pltpu.VMEM)
    any_place = pl.BlockSpec(memory_space=pl.ANY)
    scalars = pl.BlockSpec(memory_space=pltpu.SMEM)
    plane = (rows, lanes)
    limit = pltpu.CompilerParams(vmem_limit_bytes=WIDE_BYTES)

    zed_shape = pltpu.VMEM((cells,) + plane, f32)
    held = pltpu.VMEM((8, cells) + plane, f32)

    def swap_zed(zed, core):
        pairs = [(x * gz + z, x * gz + (z + 1) % gz) for x in range(core, gx, 2) for z in range(gz)]
        return pltpu.with_memory_space_constraint(lax.ppermute(zed, ("gx", "gz"), pairs), pltpu.VMEM)

    packed, zed = pl.pallas_call(
        pack_kernel,
        out_shape=[like(*sent), zed_shape],
        in_specs=[far, far],
        out_specs=[far, near],
        scratch_shapes=[held, pltpu.SemaphoreType.DMA((8,)), pltpu.SemaphoreType.DMA((8,))],
        compiler_params=limit,
    )(fields, cotangent)

    z_scratch = [
        pltpu.VMEM((4, cells) + plane, f32),
        pltpu.VMEM((4, cells) + plane, f32),
        pltpu.VMEM((3, cells) + plane, f32),
        pltpu.SemaphoreType.DMA((3,)),
    ]
    part = pltpu.VMEM((4, cells) + plane, f32)
    cost = pl.CostEstimate(flops=2 * 10**7, bytes_accessed=6 * 10**6, transcendentals=0)

    packed, res, adj, zed_later = pl.pallas_call(
        functools.partial(early_z_kernel, points),
        out_shape=[like(*sent), part, part, zed_shape],
        in_specs=[scalars] * 2 + [far] * 3 + [near, far, near],
        out_specs=[far, near, near, near],
        scratch_shapes=z_scratch,
        input_output_aliases={6: 0, 7: 3},
        cost_estimate=cost,
        compiler_params=limit,
    )(core_at, at, fields, previous, cotangent, swap_zed(zed, 1), packed, zed)
    gathered = exchange(packed)

    res, adj = pl.pallas_call(
        functools.partial(late_z_kernel, points),
        out_shape=[part, part],
        in_specs=[scalars] * 2 + [far] * 3 + [near] * 3,
        scratch_shapes=z_scratch,
        input_output_aliases={6: 0, 7: 1},
        cost_estimate=cost,
        compiler_params=limit,
    )(core_at, at, fields, previous, cotangent, swap_zed(zed_later, 0), res, adj)

    matrices = [first, second, np.ascontiguousarray(first.T), np.ascontiguousarray(second.T), weight]
    resident = pl.BlockSpec(memory_space=pltpu.VMEM)
    lined = pl.pallas_call(
        lines_kernel,
        out_shape=like(groups, 8, rows, lanes),
        in_specs=[resident] * 7,
        out_specs=pl.BlockSpec(memory_space=pltpu.HBM),
        scratch_shapes=[pltpu.VMEM((8, groups, rows, lanes), f32), pltpu.SemaphoreType.DMA((8,))],
        cost_estimate=pl.CostEstimate(
            flops=2 * points * points * lanes * 14 * 6, bytes_accessed=4 * 10**6, transcendentals=0
        ),
        compiler_params=pltpu.CompilerParams(vmem_limit_bytes=VMEM_BYTES),
    )(*[jnp.asarray(m) for m in matrices], gathered, res)
    face = pltpu.VMEM((8, 4) + plane, f32)
    last, lead = pl.pallas_call(
        faces_kernel,
        out_shape=[face, face],
        in_specs=[far] * 2 + [any_place],
        out_specs=[near] * 2,
        scratch_shapes=[pltpu.SemaphoreType.DMA((4,))],
        compiler_params=limit,
    )(fields, cotangent, lined)
    before = lax.ppermute(last, "gx", [(i, (i + 1) % gx) for i in range(gx)])
    after = lax.ppermute(lead, "gx", [((i + 1) % gx, i) for i in range(gx)])
    res, adj = pl.pallas_call(
        functools.partial(along_x_kernel, points),
        out_shape=[part, part],
        in_specs=[scalars] + [far] * 2 + [near] * 4,
        scratch_shapes=[
            pltpu.VMEM((11, cells + 8) + plane, f32),
            pltpu.VMEM((4, cells + 8) + plane, f32),
            pltpu.SemaphoreType.DMA((6,)),
        ],
        input_output_aliases={5: 0, 6: 1},
        cost_estimate=cost,
        compiler_params=limit,
    )(at, fields, cotangent, before, after, res, adj)

    back = exchange(lined)
    block = like(4, cells, rows, lanes)
    residual, adjoint = call(add_kernel, [block, block], [res, adj, back], 10**6)
    return residual, adjoint


def solution(mesh):
    spec = P(None, "gx", "gy", "gz")
    return jax.shard_map(
        per_device, mesh=mesh, in_specs=(spec,) * 3, out_specs=(spec,) * 2, check_vma=False
    )
```

```python
import functools
import math

import jax
import jax.numpy as jnp
import numpy as np
from jax import lax
from jax.experimental import pallas as pl
from jax.experimental.pallas import tpu as pltpu
from jax.sharding import PartitionSpec as P

NU_VALUE = 0.001
STEP_DT = 0.1
SPACE_X = 8.0 * math.pi / 512.0
SPACE_Z = 3.0 * math.pi / 512.0
first_coeffs = (0.8, -0.2, 4.0 / 105.0, -1.0 / 280.0)
second_coeffs = (1.6, -0.2, 8.0 / 315.0, -1.0 / 560.0)
center_coeff = -205.0 / 72.0
VMEM_BYTES = 48 * 1024 * 1024
WIDE_BYTES = 60 * 1024 * 1024
EXACT = lax.Precision.HIGHEST
f32 = jnp.float32


def wall_matrices(points):
    final_row = points - 1
    j = np.arange(points)
    half = math.pi / (2.0 * final_row)
    spacing = -2.0 * np.sin(half * (j[:, None] + j[None, :])) * np.sin(half * (j[:, None] - j[None, :]))
    ends = np.where((j == 0) | (j == final_row), 2.0, 1.0) * np.where(j % 2 == 0, 1.0, -1.0)
    eye = np.eye(points, dtype=bool)
    entries = np.where(eye, 0.0, ends[:, None] / ends[None, :] / np.where(eye, 1.0, spacing))
    first = entries - np.diag(entries.sum(axis=1))
    second = first @ first
    return first.astype(np.float32), second.astype(np.float32)


def wall_profile(points):
    final_row = points - 1
    j = np.arange(points)
    weight = np.sin(j * (math.pi / final_row)) ** 4
    return np.repeat(weight[:, None], 128, 1).astype(np.float32)


def call(kernel, outs, args, flops, scratch=()):
    moved = sum(4 * math.prod(a.shape) for a in (*outs, *args))
    return pl.pallas_call(
        kernel,
        out_shape=outs,
        scratch_shapes=list(scratch),
        cost_estimate=pl.CostEstimate(flops=flops, bytes_accessed=moved, transcendentals=0),
        compiler_params=pltpu.CompilerParams(vmem_limit_bytes=VMEM_BYTES),
    )(*args)


def like(*shape):
    return jax.ShapeDtypeStruct(shape, f32)


def row_profile(at_ref, points, shape):
    row = at_ref[0] * shape[0] + lax.broadcasted_iota(jnp.int32, shape, 0)
    weight = jnp.sin(row.astype(f32) * (math.pi / (points - 1))) ** 4
    wall = jnp.where((row == 0) | (row == points - 1), 1.0, 0.0).astype(f32)
    return weight, wall


def load(pairs, sems):
    copies = [pltpu.make_async_copy(src, dst, sems.at[i]) for i, (src, dst) in enumerate(pairs)]
    for copy in copies:
        copy.start()
    for copy in copies:
        copy.wait()


def faces_kernel(fields_any, cot_any, _token, last_out, lead_out, sems):
    cells = fields_any.shape[1]
    load(
        [
            (fields_any.at[:, cells - 4 : cells], last_out.at[0:4]),
            (cot_any.at[:, cells - 4 : cells], last_out.at[4:8]),
            (fields_any.at[:, 0:4], lead_out.at[0:4]),
            (cot_any.at[:, 0:4], lead_out.at[4:8]),
        ],
        sems,
    )


def pack_faces(held, zed_out):
    def plane(x, _):
        lane = lax.broadcasted_iota(jnp.int32, zed_out.shape[1:], 1)
        total = jnp.zeros(zed_out.shape[1:], f32)
        for c in range(8):
            moved = pltpu.roll(held[c, x], 4 + 8 * c, 1)
            total = jnp.where((lane >= 8 * c) & (lane < 8 * c + 8), moved, total)
        zed_out[x] = total
        return 0

    lax.fori_loop(0, zed_out.shape[0], plane, 0, unroll=4)


def pack_kernel(fields_any, cot_any, sent_out, zed_out, held, in_sems, out_sems):
    ins, outs = [], []
    for c in range(4):
        for ref, slot in ((fields_any, c), (cot_any, 4 + c)):
            ins.append(pltpu.make_async_copy(ref.at[c], held.at[slot], in_sems.at[slot]))
            outs.append(pltpu.make_async_copy(held.at[slot], sent_out.at[:, slot], out_sems.at[slot]))
    for copy in ins:
        copy.start()
    for arrived, leaving in zip(ins, outs):
        arrived.wait()
        leaving.start()

    pack_faces(held, zed_out)
    for copy in outs:
        copy.wait()


def stencils(values, space, need_first, need_second):
    first = second = None
    if need_first:
        for k in range(4):
            term = (first_coeffs[k] / space) * (values[5 + k] - values[3 - k])
            first = term if first is None else first + term
    if need_second:
        second = (center_coeff / (space * space)) * values[4]
        for k in range(4):
            second = second + (second_coeffs[k] / (space * space)) * (values[5 + k] + values[3 - k])
    return first, second


def along_z_work(
    core, points, core_ref, at_ref, fields_any, prev_any, cot_any, zed_ref,
    res_ref, adj_ref, field_ref, cot_ref, prev_ref, sems,
):
    cells, rows, lanes = fields_any.shape[1:]

    @pl.when(core_ref[0] % 2 == core)
    def _():
        load([(fields_any, field_ref), (cot_any, cot_ref), (prev_any, prev_ref)], sems)
        weight, wall = row_profile(at_ref, points, (rows, lanes))

        def plane(x, _):
            lane = lax.broadcasted_iota(jnp.int32, (rows, lanes), 1)
            packed = zed_ref[x]
            u = [field_ref[c, x] for c in range(4)]
            w = [weight * cot_ref[c, x] for c in range(4)]
            far = [pltpu.roll(packed, (lanes - 4 - 8 * c) % lanes, 1) for c in range(8)]
            far_u = far[0:4]
            far_w = [weight * value for value in far[4:8]]

            def along(own, other, need_first, need_second):
                values = [None] * 9
                values[4] = own
                for k in range(1, 5):
                    values[4 + k] = pltpu.roll(jnp.where(lane < k, other, own), lanes - k, 1)
                    values[4 - k] = pltpu.roll(jnp.where(lane >= lanes - k, other, own), k, 1)
                return stencils(values, SPACE_Z, need_first, need_second)

            du = [along(u[c], far_u[c], True, c < 3) for c in range(4)]
            for c in range(3):
                moment = (u[c] - prev_ref[c, x]) * (1.0 / STEP_DT) + u[2] * du[c][0] - NU_VALUE * du[c][1]
                if c == 2:
                    moment = moment + du[3][0]
                res_ref[c, x] = weight * moment + wall * u[c]
            res_ref[3, x] = weight * du[2][0]
            dw = [along(w[c], far_w[c], c >= 2, c < 3) for c in range(4)]
            for c in range(3):
                flux = along(u[2] * w[c], far_u[2] * far_w[c], True, False)[0]
                total = w[c] * (1.0 / STEP_DT) - flux - NU_VALUE * dw[c][1] + wall * cot_ref[c, x]
                if c == 2:
                    stretch = w[0] * du[0][0] + w[1] * du[1][0] + w[2] * du[2][0]
                    total = total + stretch - dw[3][0]
                adj_ref[c, x] = total
            adj_ref[3, x] = -dw[2][0]
            return 0

        lax.fori_loop(0, cells, plane, 0, unroll=2)


def early_z_kernel(
    points, core_ref, at_ref, fields_any, prev_any, cot_any, zed_ref, _packed, _zed,
    _same, res_ref, adj_ref, _same_zed, *scratch,
):
    along_z_work(
        1, points, core_ref, at_ref, fields_any, prev_any, cot_any, zed_ref, res_ref, adj_ref, *scratch
    )


def late_z_kernel(
    points, core_ref, at_ref, fields_any, prev_any, cot_any, zed_ref, _res, _adj, _lined,
    res_ref, adj_ref, token_ref, *scratch,
):
    token_ref[...] = jnp.zeros_like(token_ref)
    along_z_work(
        0, points, core_ref, at_ref, fields_any, prev_any, cot_any, zed_ref, res_ref, adj_ref, *scratch
    )


def along_x_kernel(
    points, at_ref, fields_any, cot_any, before_any, after_any, _res, _adj,
    res_ref, adj_ref, ext, cot_ref, sems,
):
    cells, rows, lanes = fields_any.shape[1:]
    load(
        [
            (fields_any, ext.at[0:4, 4 : 4 + cells]),
            (before_any.at[0:4], ext.at[0:4, 0:4]),
            (after_any.at[0:4], ext.at[0:4, 4 + cells : 8 + cells]),
            (cot_any, cot_ref.at[:, 4 : 4 + cells]),
            (before_any.at[4:8], cot_ref.at[:, 0:4]),
            (after_any.at[4:8], cot_ref.at[:, 4 + cells : 8 + cells]),
        ],
        sems,
    )
    weight = row_profile(at_ref, points, (rows, lanes))[0]

    for c in range(4):
        for x in range(cells + 8):
            value = weight * cot_ref[c, x]
            ext[4 + c, x] = value
            if c < 3:
                ext[8 + c, x] = ext[0, x] * value

    def plane(x, _):
        def along(c, need_first, need_second):
            return stencils([ext[c, x + k] for k in range(9)], SPACE_X, need_first, need_second)

        u = ext[0, 4 + x]
        w = [ext[4 + c, 4 + x] for c in range(3)]
        du = [along(c, True, c < 3) for c in range(4)]
        for c in range(3):
            moment = u * du[c][0] - NU_VALUE * du[c][1]
            if c == 0:
                moment = moment + du[3][0]
            res_ref[c, x] += weight * moment
        res_ref[3, x] += weight * du[0][0]
        dw = [along(4 + c, c in (0, 3), c < 3) for c in range(4)]
        for c in range(3):
            total = -along(8 + c, True, False)[0] - NU_VALUE * dw[c][1]
            if c == 0:
                total = total + (w[0] * du[0][0] + w[1] * du[1][0] + w[2] * du[2][0]) - dw[3][0]
            adj_ref[c, x] += total
        adj_ref[3, x] += -dw[0][0]
        return 0

    lax.fori_loop(0, cells, plane, 0)


def lines(ref, c):
    groups, _, rows, lanes = ref.shape
    return ref[:, c].reshape(groups * rows, lanes)


def blocks(value, groups):
    return value.reshape(groups, value.shape[0] // groups, value.shape[1])


def product(matrix_ref, values):
    lanes = values[0].shape[1]
    wide = jnp.dot(
        matrix_ref[...], jnp.concatenate(values, axis=1), precision=EXACT, preferred_element_type=f32
    )
    return [wide[:, i * lanes : (i + 1) * lanes] for i in range(len(values))]


def lines_kernel(
    first_ref, second_ref, first_t_ref, second_t_ref, weight_ref, in_ref, _zed, out_ref, held, sems
):
    groups = in_ref.shape[0]
    weight = weight_ref[...]
    copies = []

    def send(slot, value):
        held[slot] = blocks(value, groups)
        copies.append(pltpu.make_async_copy(held.at[slot], out_ref.at[:, slot], sems.at[slot]))
        copies[-1].start()

    u = [lines(in_ref, c) for c in range(4)]
    w = [weight * lines(in_ref, 4 + c) for c in range(4)]
    slope = product(first_ref, u)
    curve = product(second_ref, u[0:3])
    for c in range(3):
        total = u[1] * slope[c] - NU_VALUE * curve[c]
        if c == 1:
            total = total + slope[3]
        send(c, weight * total)
    send(3, weight * slope[1])
    stretch = w[0] * slope[0] + w[1] * slope[1] + w[2] * slope[2]
    lifted = product(first_t_ref, [u[1] * w[0], u[1] * w[1] + w[3], u[1] * w[2], w[1]])
    send(7, lifted[3])
    bent = product(second_t_ref, w[0:3])
    for c in range(3):
        total = lifted[c] - NU_VALUE * bent[c]
        if c == 1:
            total = total + stretch
        send(4 + c, total)
    for copy in copies:
        copy.wait()


def add_kernel(res_ref, adj_ref, back_ref, res_out, adj_out):
    for c in range(4):
        res_out[c] = res_ref[c] + back_ref[:, c]
        adj_out[c] = adj_ref[c] + back_ref[:, 4 + c]


def per_device(fields, previous, cotangent):
    cells, rows, lanes = fields.shape[1:]
    groups = lax.axis_size("gy")
    points = rows * groups
    first, second = wall_matrices(points)
    weight = wall_profile(points)
    sent = (cells, 8, rows, lanes)
    gx, gz = lax.axis_size("gx"), lax.axis_size("gz")
    at = lax.axis_index("gy").astype(jnp.int32).reshape(1)
    core_at = lax.axis_index("gx").astype(jnp.int32).reshape(1)
    exchange = functools.partial(lax.all_to_all, axis_name="gy", split_axis=0, concat_axis=0, tiled=True)
    far = pl.BlockSpec(memory_space=pltpu.HBM)
    near = pl.BlockSpec(memory_space=pltpu.VMEM)
    any_place = pl.BlockSpec(memory_space=pl.ANY)
    scalars = pl.BlockSpec(memory_space=pltpu.SMEM)
    plane = (rows, lanes)
    limit = pltpu.CompilerParams(vmem_limit_bytes=WIDE_BYTES)

    zed_shape = pltpu.VMEM((cells,) + plane, f32)
    held = pltpu.VMEM((8, cells) + plane, f32)

    def swap_zed(zed, core):
        pairs = [(x * gz + z, x * gz + (z + 1) % gz) for x in range(core, gx, 2) for z in range(gz)]
        return pltpu.with_memory_space_constraint(lax.ppermute(zed, ("gx", "gz"), pairs), pltpu.VMEM)

    packed, zed = pl.pallas_call(
        pack_kernel,
        out_shape=[like(*sent), zed_shape],
        in_specs=[far, far],
        out_specs=[far, near],
        scratch_shapes=[held, pltpu.SemaphoreType.DMA((8,)), pltpu.SemaphoreType.DMA((8,))],
        compiler_params=limit,
    )(fields, cotangent)

    z_scratch = [
        pltpu.VMEM((4, cells) + plane, f32),
        pltpu.VMEM((4, cells) + plane, f32),
        pltpu.VMEM((3, cells) + plane, f32),
        pltpu.SemaphoreType.DMA((3,)),
    ]
    part = pltpu.VMEM((4, cells) + plane, f32)
    cost = pl.CostEstimate(flops=2 * 10**7, bytes_accessed=6 * 10**6, transcendentals=0)

    packed, res, adj, zed_later = pl.pallas_call(
        functools.partial(early_z_kernel, points),
        out_shape=[like(*sent), part, part, zed_shape],
        in_specs=[scalars] * 2 + [far] * 3 + [near, far, near],
        out_specs=[far, near, near, near],
        scratch_shapes=z_scratch,
        input_output_aliases={6: 0, 7: 3},
        cost_estimate=cost,
        compiler_params=limit,
    )(core_at, at, fields, previous, cotangent, swap_zed(zed, 1), packed, zed)
    gathered = exchange(packed)

    even_zed = swap_zed(zed_later, 0)
    matrices = [first, second, np.ascontiguousarray(first.T), np.ascontiguousarray(second.T), weight]
    resident = pl.BlockSpec(memory_space=pltpu.VMEM)
    lined = pl.pallas_call(
        lines_kernel,
        out_shape=like(groups, 8, rows, lanes),
        in_specs=[resident] * 7,
        out_specs=pl.BlockSpec(memory_space=pltpu.HBM),
        scratch_shapes=[pltpu.VMEM((8, groups, rows, lanes), f32), pltpu.SemaphoreType.DMA((8,))],
        cost_estimate=pl.CostEstimate(
            flops=2 * points * points * lanes * 14 * 6, bytes_accessed=4 * 10**6, transcendentals=0
        ),
        compiler_params=pltpu.CompilerParams(vmem_limit_bytes=VMEM_BYTES),
    )(*[jnp.asarray(m) for m in matrices], gathered, even_zed)
    res, adj, token = pl.pallas_call(
        functools.partial(late_z_kernel, points),
        out_shape=[part, part, pltpu.VMEM((8, lanes), f32)],
        in_specs=[scalars] * 2 + [far] * 3 + [near] * 3 + [far],
        scratch_shapes=z_scratch,
        input_output_aliases={6: 0, 7: 1},
        cost_estimate=cost,
        compiler_params=limit,
    )(core_at, at, fields, previous, cotangent, even_zed, res, adj, lined)

    face = pltpu.VMEM((8, 4) + plane, f32)
    last, lead = pl.pallas_call(
        faces_kernel,
        out_shape=[face, face],
        in_specs=[far] * 2 + [near],
        out_specs=[near] * 2,
        scratch_shapes=[pltpu.SemaphoreType.DMA((4,))],
        compiler_params=limit,
    )(fields, cotangent, token)
    before = lax.ppermute(last, "gx", [(i, (i + 1) % gx) for i in range(gx)])
    after = lax.ppermute(lead, "gx", [((i + 1) % gx, i) for i in range(gx)])
    res, adj = pl.pallas_call(
        functools.partial(along_x_kernel, points),
        out_shape=[part, part],
        in_specs=[scalars] + [far] * 2 + [near] * 4,
        scratch_shapes=[
            pltpu.VMEM((11, cells + 8) + plane, f32),
            pltpu.VMEM((4, cells + 8) + plane, f32),
            pltpu.SemaphoreType.DMA((6,)),
        ],
        input_output_aliases={5: 0, 6: 1},
        cost_estimate=cost,
        compiler_params=limit,
    )(at, fields, cotangent, *(pltpu.with_memory_space_constraint(v, pltpu.VMEM) for v in (before, after)), res, adj)

    back = exchange(lined)
    block = like(4, cells, rows, lanes)
    residual, adjoint = call(add_kernel, [block, block], [res, adj, back], 10**6)
    return residual, adjoint


def solution(mesh):
    spec = P(None, "gx", "gy", "gz")
    return jax.shard_map(
        per_device, mesh=mesh, in_specs=(spec,) * 3, out_specs=(spec,) * 2, check_vma=False
    )
```

```python
import functools
import math

import jax
import jax.numpy as jnp
import numpy as np
from jax import lax
from jax.experimental import pallas as pl
from jax.experimental.pallas import tpu as pltpu
from jax.sharding import PartitionSpec as P

NU_VALUE = 0.001
STEP_DT = 0.1
SPACE_X = 8.0 * math.pi / 512.0
SPACE_Z = 3.0 * math.pi / 512.0
first_coeffs = (0.8, -0.2, 4.0 / 105.0, -1.0 / 280.0)
second_coeffs = (1.6, -0.2, 8.0 / 315.0, -1.0 / 560.0)
center_coeff = -205.0 / 72.0
VMEM_BYTES = 48 * 1024 * 1024
WIDE_BYTES = 60 * 1024 * 1024
EXACT = lax.Precision.HIGHEST
f32 = jnp.float32


def wall_matrices(points):
    final_row = points - 1
    j = np.arange(points)
    half = math.pi / (2.0 * final_row)
    spacing = -2.0 * np.sin(half * (j[:, None] + j[None, :])) * np.sin(half * (j[:, None] - j[None, :]))
    ends = np.where((j == 0) | (j == final_row), 2.0, 1.0) * np.where(j % 2 == 0, 1.0, -1.0)
    eye = np.eye(points, dtype=bool)
    entries = np.where(eye, 0.0, ends[:, None] / ends[None, :] / np.where(eye, 1.0, spacing))
    first = entries - np.diag(entries.sum(axis=1))
    second = first @ first
    return first.astype(np.float32), second.astype(np.float32)


def wall_profile(points):
    final_row = points - 1
    j = np.arange(points)
    weight = np.sin(j * (math.pi / final_row)) ** 4
    return np.repeat(weight[:, None], 128, 1).astype(np.float32)


def call(kernel, outs, args, flops, scratch=()):
    moved = sum(4 * math.prod(a.shape) for a in (*outs, *args))
    return pl.pallas_call(
        kernel,
        out_shape=outs,
        scratch_shapes=list(scratch),
        cost_estimate=pl.CostEstimate(flops=flops, bytes_accessed=moved, transcendentals=0),
        compiler_params=pltpu.CompilerParams(vmem_limit_bytes=VMEM_BYTES),
    )(*args)


def like(*shape):
    return jax.ShapeDtypeStruct(shape, f32)


def row_profile(at_ref, points, shape):
    row = at_ref[0] * shape[0] + lax.broadcasted_iota(jnp.int32, shape, 0)
    weight = jnp.sin(row.astype(f32) * (math.pi / (points - 1))) ** 4
    wall = jnp.where((row == 0) | (row == points - 1), 1.0, 0.0).astype(f32)
    return weight, wall


def load(pairs, sems):
    copies = [pltpu.make_async_copy(src, dst, sems.at[i]) for i, (src, dst) in enumerate(pairs)]
    for copy in copies:
        copy.start()
    for copy in copies:
        copy.wait()


def z_faces(held, zed_out):
    half = zed_out.shape[0]

    def plane(x, _):
        lane = lax.broadcasted_iota(jnp.int32, zed_out.shape[1:], 1)
        total = jnp.zeros(zed_out.shape[1:], f32)
        for c in range(8):
            for side in range(2):
                at = 8 * c + 64 * side
                moved = pltpu.roll(held[c, x + half * side], 4 + at, 1)
                total = jnp.where((lane >= at) & (lane < at + 8), moved, total)
        zed_out[x] = total
        return 0

    lax.fori_loop(0, half, plane, 0, unroll=2)


def pack_kernel(core_ref, fields_any, cot_any, sent_out, zed_out, last_out, lead_out, held, sems):
    cells = fields_any.shape[1]
    copies = [
        pltpu.make_async_copy(fields_any, held.at[0:4], sems.at[0]),
        pltpu.make_async_copy(cot_any, held.at[4:8], sems.at[1]),
    ]
    for copy in copies:
        copy.start()
    for part, copy in enumerate(copies):
        copy.wait()
        for c in range(4 * part, 4 * part + 4):
            sent_out[:, c] = held[c]
            last_out[c] = held[c, cells - 4 : cells]
            lead_out[c] = held[c, 0:4]

    @pl.when(core_ref[0] % 2 == 1)
    def _():
        z_faces(held, zed_out)


def late_faces_kernel(core_ref, fields_any, cot_any, _lined, zed_out, held, sems):
    @pl.when(core_ref[0] % 2 == 0)
    def _():
        load([(fields_any, held.at[0:4]), (cot_any, held.at[4:8])], sems)
        z_faces(held, zed_out)


def order_kernel(_zed, _last, _lead, _same_last, _same_lead):
    pass


def stencils(values, space, need_first, need_second):
    first = second = None
    if need_first:
        for k in range(4):
            term = (first_coeffs[k] / space) * (values[5 + k] - values[3 - k])
            first = term if first is None else first + term
    if need_second:
        second = (center_coeff / (space * space)) * values[4]
        for k in range(4):
            second = second + (second_coeffs[k] / (space * space)) * (values[5 + k] + values[3 - k])
    return first, second


def along_z_work(
    core, points, core_ref, at_ref, fields_any, prev_any, cot_any, zed_ref,
    res_ref, adj_ref, field_ref, cot_ref, prev_ref, sems,
):
    cells, rows, lanes = fields_any.shape[1:]
    half = cells // 2

    @pl.when(core_ref[0] % 2 == core)
    def _():
        load([(fields_any, field_ref), (cot_any, cot_ref), (prev_any, prev_ref)], sems)
        weight, wall = row_profile(at_ref, points, (rows, lanes))

        def plane(side, step, _):
            x = step + half * side
            lane = lax.broadcasted_iota(jnp.int32, (rows, lanes), 1)
            packed = zed_ref[step]
            u = [field_ref[c, x] for c in range(4)]
            w = [weight * cot_ref[c, x] for c in range(4)]
            far = [pltpu.roll(packed, (lanes - 4 - 8 * c - 64 * side) % lanes, 1) for c in range(8)]
            far_u = far[0:4]
            far_w = [weight * value for value in far[4:8]]

            def along(own, other, need_first, need_second):
                values = [None] * 9
                values[4] = own
                for k in range(1, 5):
                    values[4 + k] = pltpu.roll(jnp.where(lane < k, other, own), lanes - k, 1)
                    values[4 - k] = pltpu.roll(jnp.where(lane >= lanes - k, other, own), k, 1)
                return stencils(values, SPACE_Z, need_first, need_second)

            du = [along(u[c], far_u[c], True, c < 3) for c in range(4)]
            for c in range(3):
                moment = (u[c] - prev_ref[c, x]) * (1.0 / STEP_DT) + u[2] * du[c][0] - NU_VALUE * du[c][1]
                if c == 2:
                    moment = moment + du[3][0]
                res_ref[c, x] = weight * moment + wall * u[c]
            res_ref[3, x] = weight * du[2][0]
            dw = [along(w[c], far_w[c], c >= 2, c < 3) for c in range(4)]
            for c in range(3):
                flux = along(u[2] * w[c], far_u[2] * far_w[c], True, False)[0]
                total = w[c] * (1.0 / STEP_DT) - flux - NU_VALUE * dw[c][1] + wall * cot_ref[c, x]
                if c == 2:
                    stretch = w[0] * du[0][0] + w[1] * du[1][0] + w[2] * du[2][0]
                    total = total + stretch - dw[3][0]
                adj_ref[c, x] = total
            adj_ref[3, x] = -dw[2][0]
            return 0

        for side in range(2):
            lax.fori_loop(0, half, functools.partial(plane, side), 0, unroll=1 + (core == 0))


def early_z_kernel(
    points, core_ref, at_ref, fields_any, prev_any, cot_any, zed_ref, _packed,
    _same, res_ref, adj_ref, *scratch,
):
    along_z_work(
        1, points, core_ref, at_ref, fields_any, prev_any, cot_any, zed_ref, res_ref, adj_ref, *scratch
    )


def late_z_kernel(
    points, core_ref, at_ref, fields_any, prev_any, cot_any, zed_ref, _res, _adj,
    res_ref, adj_ref, *scratch,
):
    along_z_work(
        0, points, core_ref, at_ref, fields_any, prev_any, cot_any, zed_ref, res_ref, adj_ref, *scratch
    )


def along_x_kernel(
    points, at_ref, fields_any, cot_any, before_any, after_any, _res, _adj,
    res_ref, adj_ref, ext, cot_ref, sems,
):
    cells, rows, lanes = fields_any.shape[1:]
    load(
        [
            (fields_any, ext.at[0:4, 4 : 4 + cells]),
            (before_any.at[0:4], ext.at[0:4, 0:4]),
            (after_any.at[0:4], ext.at[0:4, 4 + cells : 8 + cells]),
            (cot_any, cot_ref.at[:, 4 : 4 + cells]),
            (before_any.at[4:8], cot_ref.at[:, 0:4]),
            (after_any.at[4:8], cot_ref.at[:, 4 + cells : 8 + cells]),
        ],
        sems,
    )
    weight = row_profile(at_ref, points, (rows, lanes))[0]

    for c in range(4):
        for x in range(cells + 8):
            value = weight * cot_ref[c, x]
            ext[4 + c, x] = value
            if c < 3:
                ext[8 + c, x] = ext[0, x] * value

    def plane(x, _):
        def along(c, need_first, need_second):
            return stencils([ext[c, x + k] for k in range(9)], SPACE_X, need_first, need_second)

        u = ext[0, 4 + x]
        w = [ext[4 + c, 4 + x] for c in range(3)]
        du = [along(c, True, c < 3) for c in range(4)]
        for c in range(3):
            moment = u * du[c][0] - NU_VALUE * du[c][1]
            if c == 0:
                moment = moment + du[3][0]
            res_ref[c, x] += weight * moment
        res_ref[3, x] += weight * du[0][0]
        dw = [along(4 + c, c in (0, 3), c < 3) for c in range(4)]
        for c in range(3):
            total = -along(8 + c, True, False)[0] - NU_VALUE * dw[c][1]
            if c == 0:
                total = total + (w[0] * du[0][0] + w[1] * du[1][0] + w[2] * du[2][0]) - dw[3][0]
            adj_ref[c, x] += total
        adj_ref[3, x] += -dw[0][0]
        return 0

    lax.fori_loop(0, cells, plane, 0)


def lines(ref, c):
    groups, _, rows, lanes = ref.shape
    return ref[:, c].reshape(groups * rows, lanes)


def blocks(value, groups):
    return value.reshape(groups, value.shape[0] // groups, value.shape[1])


def product(matrix_ref, values):
    lanes = values[0].shape[1]
    wide = jnp.dot(
        matrix_ref[...], jnp.concatenate(values, axis=1), precision=EXACT, preferred_element_type=f32
    )
    return [wide[:, i * lanes : (i + 1) * lanes] for i in range(len(values))]


def lines_kernel(
    first_ref, second_ref, first_t_ref, second_t_ref, weight_ref, in_ref, out_ref, held, sems
):
    groups = in_ref.shape[0]
    weight = weight_ref[...]
    copies = []

    def send(slot, value):
        held[slot] = blocks(value, groups)
        copies.append(pltpu.make_async_copy(held.at[slot], out_ref.at[:, slot], sems.at[slot]))
        copies[-1].start()

    u = [lines(in_ref, c) for c in range(4)]
    w = [weight * lines(in_ref, 4 + c) for c in range(4)]
    slope = product(first_ref, u)
    curve = product(second_ref, u[0:3])
    for c in range(3):
        total = u[1] * slope[c] - NU_VALUE * curve[c]
        if c == 1:
            total = total + slope[3]
        send(c, weight * total)
    send(3, weight * slope[1])
    stretch = w[0] * slope[0] + w[1] * slope[1] + w[2] * slope[2]
    lifted = product(first_t_ref, [u[1] * w[0], u[1] * w[1] + w[3], u[1] * w[2], w[1]])
    send(7, lifted[3])
    bent = product(second_t_ref, w[0:3])
    for c in range(3):
        total = lifted[c] - NU_VALUE * bent[c]
        if c == 1:
            total = total + stretch
        send(4 + c, total)
    for copy in copies:
        copy.wait()


def add_kernel(res_ref, adj_ref, back_ref, res_out, adj_out):
    for c in range(4):
        res_out[c] = res_ref[c] + back_ref[:, c]
        adj_out[c] = adj_ref[c] + back_ref[:, 4 + c]


def per_device(fields, previous, cotangent):
    cells, rows, lanes = fields.shape[1:]
    groups = lax.axis_size("gy")
    points = rows * groups
    first, second = wall_matrices(points)
    weight = wall_profile(points)
    sent = (cells, 8, rows, lanes)
    gx, gz = lax.axis_size("gx"), lax.axis_size("gz")
    at = lax.axis_index("gy").astype(jnp.int32).reshape(1)
    core_at = lax.axis_index("gx").astype(jnp.int32).reshape(1)
    exchange = functools.partial(lax.all_to_all, axis_name="gy", split_axis=0, concat_axis=0, tiled=True)
    far = pl.BlockSpec(memory_space=pltpu.HBM)
    near = pl.BlockSpec(memory_space=pltpu.VMEM)
    any_place = pl.BlockSpec(memory_space=pl.ANY)
    scalars = pl.BlockSpec(memory_space=pltpu.SMEM)
    plane = (rows, lanes)
    limit = pltpu.CompilerParams(vmem_limit_bytes=WIDE_BYTES)

    zed_shape = pltpu.VMEM((cells // 2,) + plane, f32)
    face = pltpu.VMEM((8, 4) + plane, f32)

    def swap_zed(zed, core):
        pairs = [(x * gz + z, x * gz + (z + 1) % gz) for x in range(core, gx, 2) for z in range(gz)]
        return pltpu.with_memory_space_constraint(lax.ppermute(zed, ("gx", "gz"), pairs), pltpu.VMEM)

    packed, zed, last, lead = pl.pallas_call(
        pack_kernel,
        out_shape=[pltpu.VMEM(sent, f32), zed_shape, face, face],
        in_specs=[scalars, far, far],
        out_specs=[near] * 4,
        scratch_shapes=[pltpu.VMEM((8, cells) + plane, f32), pltpu.SemaphoreType.DMA((2,))],
        compiler_params=limit,
    )(core_at, fields, cotangent)

    z_scratch = [
        pltpu.VMEM((4, cells) + plane, f32),
        pltpu.VMEM((4, cells) + plane, f32),
        pltpu.VMEM((3, cells) + plane, f32),
        pltpu.SemaphoreType.DMA((3,)),
    ]
    part = pltpu.VMEM((4, cells) + plane, f32)
    cost = pl.CostEstimate(flops=2 * 10**7, bytes_accessed=6 * 10**6, transcendentals=0)

    packed, res, adj = pl.pallas_call(
        functools.partial(early_z_kernel, points),
        out_shape=[pltpu.VMEM(sent, f32), part, part],
        in_specs=[scalars] * 2 + [far] * 3 + [near] * 2,
        out_specs=[near] * 3,
        scratch_shapes=z_scratch,
        input_output_aliases={6: 0},
        cost_estimate=cost,
        compiler_params=limit,
    )(core_at, at, fields, previous, cotangent, swap_zed(zed, 1), packed)
    gathered = exchange(packed)

    matrices = [first, second, np.ascontiguousarray(first.T), np.ascontiguousarray(second.T), weight]
    resident = pl.BlockSpec(memory_space=pltpu.VMEM)
    lined = pl.pallas_call(
        lines_kernel,
        out_shape=like(groups, 8, rows, lanes),
        in_specs=[resident] * 6,
        out_specs=far,
        scratch_shapes=[pltpu.VMEM((8, groups, rows, lanes), f32), pltpu.SemaphoreType.DMA((8,))],
        cost_estimate=pl.CostEstimate(
            flops=2 * points * points * lanes * 14 * 6, bytes_accessed=4 * 10**6, transcendentals=0
        ),
        compiler_params=pltpu.CompilerParams(vmem_limit_bytes=VMEM_BYTES),
    )(*[jnp.asarray(m) for m in matrices], gathered)

    zed_later = pl.pallas_call(
        late_faces_kernel,
        out_shape=zed_shape,
        in_specs=[scalars] + [far] * 3,
        scratch_shapes=[pltpu.VMEM((8, cells) + plane, f32), pltpu.SemaphoreType.DMA((2,))],
        cost_estimate=cost,
        compiler_params=limit,
    )(core_at, fields, cotangent, lined)
    even_zed = swap_zed(zed_later, 0)
    last, lead = pl.pallas_call(
        order_kernel,
        out_shape=[face, face],
        in_specs=[near] * 3,
        input_output_aliases={1: 0, 2: 1},
        compiler_params=limit,
    )(even_zed, last, lead)
    res, adj = pl.pallas_call(
        functools.partial(late_z_kernel, points),
        out_shape=[part, part],
        in_specs=[scalars] * 2 + [far] * 3 + [near] * 3,
        scratch_shapes=z_scratch,
        input_output_aliases={6: 0, 7: 1},
        cost_estimate=cost,
        compiler_params=limit,
    )(core_at, at, fields, previous, cotangent, even_zed, res, adj)

    before = lax.ppermute(last, "gx", [(i, (i + 1) % gx) for i in range(gx)])
    after = lax.ppermute(lead, "gx", [((i + 1) % gx, i) for i in range(gx)])
    res, adj = pl.pallas_call(
        functools.partial(along_x_kernel, points),
        out_shape=[part, part],
        in_specs=[scalars] + [far] * 2 + [near] * 4,
        scratch_shapes=[
            pltpu.VMEM((11, cells + 8) + plane, f32),
            pltpu.VMEM((4, cells + 8) + plane, f32),
            pltpu.SemaphoreType.DMA((6,)),
        ],
        input_output_aliases={5: 0, 6: 1},
        cost_estimate=cost,
        compiler_params=limit,
    )(at, fields, cotangent, *(pltpu.with_memory_space_constraint(v, pltpu.VMEM) for v in (before, after)), res, adj)

    back = exchange(lined)
    block = like(4, cells, rows, lanes)
    residual, adjoint = call(add_kernel, [block, block], [res, adj, back], 10**6)
    return residual, adjoint


def solution(mesh):
    spec = P(None, "gx", "gy", "gz")
    return jax.shard_map(
        per_device, mesh=mesh, in_specs=(spec,) * 3, out_specs=(spec,) * 2, check_vma=False
    )
```

```python
import functools
import math

import jax
import jax.numpy as jnp
import numpy as np
from jax import lax
from jax.experimental import pallas as pl
from jax.experimental.pallas import tpu as pltpu
from jax.sharding import PartitionSpec as P

NU_VALUE = 0.001
STEP_DT = 0.1
SPACE_X = 8.0 * math.pi / 512.0
SPACE_Z = 3.0 * math.pi / 512.0
first_coeffs = (0.8, -0.2, 4.0 / 105.0, -1.0 / 280.0)
second_coeffs = (1.6, -0.2, 8.0 / 315.0, -1.0 / 560.0)
center_coeff = -205.0 / 72.0
VMEM_BYTES = 48 * 1024 * 1024
WIDE_BYTES = 60 * 1024 * 1024
EXACT = lax.Precision.HIGHEST
f32 = jnp.float32


def wall_matrices(points):
    final_row = points - 1
    j = np.arange(points)
    half = math.pi / (2.0 * final_row)
    spacing = -2.0 * np.sin(half * (j[:, None] + j[None, :])) * np.sin(half * (j[:, None] - j[None, :]))
    ends = np.where((j == 0) | (j == final_row), 2.0, 1.0) * np.where(j % 2 == 0, 1.0, -1.0)
    eye = np.eye(points, dtype=bool)
    entries = np.where(eye, 0.0, ends[:, None] / ends[None, :] / np.where(eye, 1.0, spacing))
    first = entries - np.diag(entries.sum(axis=1))
    second = first @ first
    return first.astype(np.float32), second.astype(np.float32)


def wall_profile(points):
    final_row = points - 1
    j = np.arange(points)
    weight = np.sin(j * (math.pi / final_row)) ** 4
    return np.repeat(weight[:, None], 128, 1).astype(np.float32)


def call(kernel, outs, args, flops, scratch=()):
    moved = sum(4 * math.prod(a.shape) for a in (*outs, *args))
    return pl.pallas_call(
        kernel,
        out_shape=outs,
        scratch_shapes=list(scratch),
        cost_estimate=pl.CostEstimate(flops=flops, bytes_accessed=moved, transcendentals=0),
        compiler_params=pltpu.CompilerParams(vmem_limit_bytes=VMEM_BYTES),
    )(*args)


def like(*shape):
    return jax.ShapeDtypeStruct(shape, f32)


def row_profile(at_ref, points, shape):
    row = at_ref[0] * shape[0] + lax.broadcasted_iota(jnp.int32, shape, 0)
    weight = jnp.sin(row.astype(f32) * (math.pi / (points - 1))) ** 4
    wall = jnp.where((row == 0) | (row == points - 1), 1.0, 0.0).astype(f32)
    return weight, wall


def load(pairs, sems):
    copies = [pltpu.make_async_copy(src, dst, sems.at[i]) for i, (src, dst) in enumerate(pairs)]
    for copy in copies:
        copy.start()
    for copy in copies:
        copy.wait()


def z_faces(held, zed_out):
    half = zed_out.shape[0]

    def plane(x, _):
        lane = lax.broadcasted_iota(jnp.int32, zed_out.shape[1:], 1)
        total = jnp.zeros(zed_out.shape[1:], f32)
        for c in range(8):
            for side in range(2):
                at = 8 * c + 64 * side
                moved = pltpu.roll(held[c, x + half * side], 4 + at, 1)
                total = jnp.where((lane >= at) & (lane < at + 8), moved, total)
        zed_out[x] = total
        return 0

    lax.fori_loop(0, half, plane, 0, unroll=2)


def pack_kernel(core_ref, fields_any, cot_any, sent_out, zed_out, last_out, lead_out, held, sems):
    cells = fields_any.shape[1]
    copies = [
        pltpu.make_async_copy(fields_any, held.at[0:4], sems.at[0]),
        pltpu.make_async_copy(cot_any, held.at[4:8], sems.at[1]),
    ]
    for copy in copies:
        copy.start()
    for part, copy in enumerate(copies):
        copy.wait()
        for c in range(4 * part, 4 * part + 4):
            sent_out[:, c] = held[c]
            last_out[c] = held[c, cells - 4 : cells]
            lead_out[c] = held[c, 0:4]

    @pl.when(core_ref[0] % 2 == 1)
    def _():
        z_faces(held, zed_out)


def late_faces_kernel(core_ref, fields_any, cot_any, _lined, zed_out, held, sems):
    @pl.when(core_ref[0] % 2 == 0)
    def _():
        load([(fields_any, held.at[0:4]), (cot_any, held.at[4:8])], sems)
        z_faces(held, zed_out)


def order_kernel(_zed, _last, _lead, _same_last, _same_lead):
    pass


def stencils(values, space, need_first, need_second):
    first = second = None
    if need_first:
        for k in range(4):
            term = (first_coeffs[k] / space) * (values[5 + k] - values[3 - k])
            first = term if first is None else first + term
    if need_second:
        second = (center_coeff / (space * space)) * values[4]
        for k in range(4):
            second = second + (second_coeffs[k] / (space * space)) * (values[5 + k] + values[3 - k])
    return first, second


def along_z_work(
    core, points, core_ref, at_ref, fields_any, prev_any, cot_any, zed_ref,
    res_ref, adj_ref, field_ref, cot_ref, prev_ref, sems,
):
    cells, rows, lanes = fields_any.shape[1:]
    half = cells // 2

    @pl.when(core_ref[0] % 2 == core)
    def _():
        load([(fields_any, field_ref), (cot_any, cot_ref), (prev_any, prev_ref)], sems)
        weight, wall = row_profile(at_ref, points, (rows, lanes))

        def plane(side, step, _):
            x = step + half * side
            lane = lax.broadcasted_iota(jnp.int32, (rows, lanes), 1)
            packed = zed_ref[step]
            u = [field_ref[c, x] for c in range(4)]
            w = [weight * cot_ref[c, x] for c in range(4)]
            far = [pltpu.roll(packed, (lanes - 4 - 8 * c - 64 * side) % lanes, 1) for c in range(8)]
            far_u = far[0:4]
            far_w = [weight * value for value in far[4:8]]

            def along(own, other, need_first, need_second):
                values = [None] * 9
                values[4] = own
                for k in range(1, 5):
                    values[4 + k] = pltpu.roll(jnp.where(lane < k, other, own), lanes - k, 1)
                    values[4 - k] = pltpu.roll(jnp.where(lane >= lanes - k, other, own), k, 1)
                return stencils(values, SPACE_Z, need_first, need_second)

            du = [along(u[c], far_u[c], True, c < 3) for c in range(4)]
            for c in range(3):
                moment = (u[c] - prev_ref[c, x]) * (1.0 / STEP_DT) + u[2] * du[c][0] - NU_VALUE * du[c][1]
                if c == 2:
                    moment = moment + du[3][0]
                res_ref[c, x] = weight * moment + wall * u[c]
            res_ref[3, x] = weight * du[2][0]
            dw = [along(w[c], far_w[c], c >= 2, c < 3) for c in range(4)]
            for c in range(3):
                flux = along(u[2] * w[c], far_u[2] * far_w[c], True, False)[0]
                total = w[c] * (1.0 / STEP_DT) - flux - NU_VALUE * dw[c][1] + wall * cot_ref[c, x]
                if c == 2:
                    stretch = w[0] * du[0][0] + w[1] * du[1][0] + w[2] * du[2][0]
                    total = total + stretch - dw[3][0]
                adj_ref[c, x] = total
            adj_ref[3, x] = -dw[2][0]
            return 0

        for side in range(2):
            lax.fori_loop(0, half, functools.partial(plane, side), 0, unroll=1 + (core == 0))


def early_z_kernel(
    points, core_ref, at_ref, fields_any, prev_any, cot_any, zed_ref, _packed,
    _same, res_ref, adj_ref, *scratch,
):
    along_z_work(
        1, points, core_ref, at_ref, fields_any, prev_any, cot_any, zed_ref, res_ref, adj_ref, *scratch
    )


def late_z_kernel(
    points, core_ref, at_ref, fields_any, prev_any, cot_any, zed_ref, _res, _adj,
    res_ref, adj_ref, *scratch,
):
    along_z_work(
        0, points, core_ref, at_ref, fields_any, prev_any, cot_any, zed_ref, res_ref, adj_ref, *scratch
    )


def along_x_kernel(
    points, at_ref, fields_any, cot_any, before_any, after_any, _res, _adj,
    res_ref, adj_ref, ext, cot_ref, sems,
):
    cells, rows, lanes = fields_any.shape[1:]
    load(
        [
            (fields_any, ext.at[0:4, 4 : 4 + cells]),
            (before_any.at[0:4], ext.at[0:4, 0:4]),
            (after_any.at[0:4], ext.at[0:4, 4 + cells : 8 + cells]),
            (cot_any, cot_ref.at[:, 4 : 4 + cells]),
            (before_any.at[4:8], cot_ref.at[:, 0:4]),
            (after_any.at[4:8], cot_ref.at[:, 4 + cells : 8 + cells]),
        ],
        sems,
    )
    weight = row_profile(at_ref, points, (rows, lanes))[0]

    for c in range(4):
        for x in range(cells + 8):
            value = weight * cot_ref[c, x]
            ext[4 + c, x] = value
            if c < 3:
                ext[8 + c, x] = ext[0, x] * value

    def plane(x, _):
        def along(c, need_first, need_second):
            return stencils([ext[c, x + k] for k in range(9)], SPACE_X, need_first, need_second)

        u = ext[0, 4 + x]
        w = [ext[4 + c, 4 + x] for c in range(3)]
        du = [along(c, True, c < 3) for c in range(4)]
        for c in range(3):
            moment = u * du[c][0] - NU_VALUE * du[c][1]
            if c == 0:
                moment = moment + du[3][0]
            res_ref[c, x] += weight * moment
        res_ref[3, x] += weight * du[0][0]
        dw = [along(4 + c, c in (0, 3), c < 3) for c in range(4)]
        for c in range(3):
            total = -along(8 + c, True, False)[0] - NU_VALUE * dw[c][1]
            if c == 0:
                total = total + (w[0] * du[0][0] + w[1] * du[1][0] + w[2] * du[2][0]) - dw[3][0]
            adj_ref[c, x] += total
        adj_ref[3, x] += -dw[0][0]
        return 0

    lax.fori_loop(0, cells, plane, 0)


def lines(ref, c):
    groups, _, rows, lanes = ref.shape
    return ref[:, c].reshape(groups * rows, lanes)


def blocks(value, groups):
    return value.reshape(groups, value.shape[0] // groups, value.shape[1])


def product(matrix_ref, values):
    lanes = values[0].shape[1]
    wide = jnp.dot(
        matrix_ref[...], jnp.concatenate(values, axis=1), precision=EXACT, preferred_element_type=f32
    )
    return [wide[:, i * lanes : (i + 1) * lanes] for i in range(len(values))]


def lines_kernel(
    first_ref, second_ref, first_t_ref, second_t_ref, weight_ref, in_ref, out_ref, held, sems
):
    groups = in_ref.shape[0]
    weight = weight_ref[...]
    copies = []

    def send(slot, value):
        held[slot] = blocks(value, groups)
        copies.append(pltpu.make_async_copy(held.at[slot], out_ref.at[:, slot], sems.at[slot]))
        copies[-1].start()

    u = [lines(in_ref, c) for c in range(4)]
    w = [weight * lines(in_ref, 4 + c) for c in range(4)]
    slope_2, slope_1 = product(first_ref, [u[1], u[0]])
    press, lifted_1 = product(first_t_ref, [w[1], u[1] * w[0]])
    curve_1, curve_3 = product(second_ref, [u[0], u[2]])
    send(0, weight * (u[1] * slope_1 - NU_VALUE * curve_1))
    send(3, weight * slope_2)
    send(7, press)
    slope_3, joint = product(first_ref, [u[2], u[3] - NU_VALUE * slope_2])
    send(1, weight * (u[1] * slope_2 + joint))
    send(2, weight * (u[1] * slope_3 - NU_VALUE * curve_3))
    stretch = w[0] * slope_1 + w[1] * slope_2 + w[2] * slope_3
    bent_1, bent_3 = product(second_t_ref, [w[0], w[2]])
    send(4, lifted_1 - NU_VALUE * bent_1)
    lifted_2, lifted_3 = product(first_t_ref, [u[1] * w[1] + w[3] - NU_VALUE * press, u[1] * w[2]])
    send(5, lifted_2 + stretch)
    send(6, lifted_3 - NU_VALUE * bent_3)
    for copy in copies:
        copy.wait()


def add_kernel(res_ref, adj_ref, back_ref, res_out, adj_out):
    for c in range(4):
        res_out[c] = res_ref[c] + back_ref[:, c]
        adj_out[c] = adj_ref[c] + back_ref[:, 4 + c]


def per_device(fields, previous, cotangent):
    cells, rows, lanes = fields.shape[1:]
    groups = lax.axis_size("gy")
    points = rows * groups
    first, second = wall_matrices(points)
    weight = wall_profile(points)
    sent = (cells, 8, rows, lanes)
    gx, gz = lax.axis_size("gx"), lax.axis_size("gz")
    at = lax.axis_index("gy").astype(jnp.int32).reshape(1)
    core_at = lax.axis_index("gx").astype(jnp.int32).reshape(1)
    exchange = functools.partial(lax.all_to_all, axis_name="gy", split_axis=0, concat_axis=0, tiled=True)
    far = pl.BlockSpec(memory_space=pltpu.HBM)
    near = pl.BlockSpec(memory_space=pltpu.VMEM)
    any_place = pl.BlockSpec(memory_space=pl.ANY)
    scalars = pl.BlockSpec(memory_space=pltpu.SMEM)
    plane = (rows, lanes)
    limit = pltpu.CompilerParams(vmem_limit_bytes=WIDE_BYTES)

    zed_shape = pltpu.VMEM((cells // 2,) + plane, f32)
    face = pltpu.VMEM((8, 4) + plane, f32)

    def swap_zed(zed, core):
        pairs = [(x * gz + z, x * gz + (z + 1) % gz) for x in range(core, gx, 2) for z in range(gz)]
        return pltpu.with_memory_space_constraint(lax.ppermute(zed, ("gx", "gz"), pairs), pltpu.VMEM)

    packed, zed, last, lead = pl.pallas_call(
        pack_kernel,
        out_shape=[pltpu.VMEM(sent, f32), zed_shape, face, face],
        in_specs=[scalars, far, far],
        out_specs=[near] * 4,
        scratch_shapes=[pltpu.VMEM((8, cells) + plane, f32), pltpu.SemaphoreType.DMA((2,))],
        compiler_params=limit,
    )(core_at, fields, cotangent)

    z_scratch = [
        pltpu.VMEM((4, cells) + plane, f32),
        pltpu.VMEM((4, cells) + plane, f32),
        pltpu.VMEM((3, cells) + plane, f32),
        pltpu.SemaphoreType.DMA((3,)),
    ]
    part = pltpu.VMEM((4, cells) + plane, f32)
    cost = pl.CostEstimate(flops=2 * 10**7, bytes_accessed=6 * 10**6, transcendentals=0)

    packed, res, adj = pl.pallas_call(
        functools.partial(early_z_kernel, points),
        out_shape=[pltpu.VMEM(sent, f32), part, part],
        in_specs=[scalars] * 2 + [far] * 3 + [near] * 2,
        out_specs=[near] * 3,
        scratch_shapes=z_scratch,
        input_output_aliases={6: 0},
        cost_estimate=cost,
        compiler_params=limit,
    )(core_at, at, fields, previous, cotangent, swap_zed(zed, 1), packed)
    gathered = exchange(packed)

    matrices = [first, second, np.ascontiguousarray(first.T), np.ascontiguousarray(second.T), weight]
    resident = pl.BlockSpec(memory_space=pltpu.VMEM)
    lined = pl.pallas_call(
        lines_kernel,
        out_shape=like(groups, 8, rows, lanes),
        in_specs=[resident] * 6,
        out_specs=far,
        scratch_shapes=[pltpu.VMEM((8, groups, rows, lanes), f32), pltpu.SemaphoreType.DMA((8,))],
        cost_estimate=pl.CostEstimate(
            flops=2 * points * points * lanes * 14 * 6, bytes_accessed=4 * 10**6, transcendentals=0
        ),
        compiler_params=pltpu.CompilerParams(vmem_limit_bytes=VMEM_BYTES),
    )(*[jnp.asarray(m) for m in matrices], gathered)

    zed_later = pl.pallas_call(
        late_faces_kernel,
        out_shape=zed_shape,
        in_specs=[scalars] + [far] * 3,
        scratch_shapes=[pltpu.VMEM((8, cells) + plane, f32), pltpu.SemaphoreType.DMA((2,))],
        cost_estimate=cost,
        compiler_params=limit,
    )(core_at, fields, cotangent, lined)
    even_zed = swap_zed(zed_later, 0)
    last, lead = pl.pallas_call(
        order_kernel,
        out_shape=[face, face],
        in_specs=[near] * 3,
        input_output_aliases={1: 0, 2: 1},
        compiler_params=limit,
    )(even_zed, last, lead)
    res, adj = pl.pallas_call(
        functools.partial(late_z_kernel, points),
        out_shape=[part, part],
        in_specs=[scalars] * 2 + [far] * 3 + [near] * 3,
        scratch_shapes=z_scratch,
        input_output_aliases={6: 0, 7: 1},
        cost_estimate=cost,
        compiler_params=limit,
    )(core_at, at, fields, previous, cotangent, even_zed, res, adj)

    before = lax.ppermute(last, "gx", [(i, (i + 1) % gx) for i in range(gx)])
    after = lax.ppermute(lead, "gx", [((i + 1) % gx, i) for i in range(gx)])
    res, adj = pl.pallas_call(
        functools.partial(along_x_kernel, points),
        out_shape=[part, part],
        in_specs=[scalars] + [far] * 2 + [near] * 4,
        scratch_shapes=[
            pltpu.VMEM((11, cells + 8) + plane, f32),
            pltpu.VMEM((4, cells + 8) + plane, f32),
            pltpu.SemaphoreType.DMA((6,)),
        ],
        input_output_aliases={5: 0, 6: 1},
        cost_estimate=cost,
        compiler_params=limit,
    )(at, fields, cotangent, *(pltpu.with_memory_space_constraint(v, pltpu.VMEM) for v in (before, after)), res, adj)

    back = exchange(lined)
    block = like(4, cells, rows, lanes)
    residual, adjoint = call(add_kernel, [block, block], [res, adj, back], 10**6)
    return residual, adjoint


def solution(mesh):
    spec = P(None, "gx", "gy", "gz")
    return jax.shard_map(
        per_device, mesh=mesh, in_specs=(spec,) * 3, out_specs=(spec,) * 2, check_vma=False
    )
```

```python
import functools
import math

import jax
import jax.numpy as jnp
import numpy as np
from jax import lax
from jax.experimental import pallas as pl
from jax.experimental.pallas import tpu as pltpu
from jax.sharding import PartitionSpec as P

NU_VALUE = 0.001
STEP_DT = 0.1
SPACE_X = 8.0 * math.pi / 512.0
SPACE_Z = 3.0 * math.pi / 512.0
first_coeffs = (0.8, -0.2, 4.0 / 105.0, -1.0 / 280.0)
second_coeffs = (1.6, -0.2, 8.0 / 315.0, -1.0 / 560.0)
center_coeff = -205.0 / 72.0
VMEM_BYTES = 48 * 1024 * 1024
WIDE_BYTES = 60 * 1024 * 1024
EXACT = lax.Precision.HIGHEST
f32 = jnp.float32


def wall_matrices(points):
    final_row = points - 1
    j = np.arange(points)
    half = math.pi / (2.0 * final_row)
    spacing = -2.0 * np.sin(half * (j[:, None] + j[None, :])) * np.sin(half * (j[:, None] - j[None, :]))
    ends = np.where((j == 0) | (j == final_row), 2.0, 1.0) * np.where(j % 2 == 0, 1.0, -1.0)
    eye = np.eye(points, dtype=bool)
    entries = np.where(eye, 0.0, ends[:, None] / ends[None, :] / np.where(eye, 1.0, spacing))
    first = entries - np.diag(entries.sum(axis=1))
    second = first @ first
    return first.astype(np.float32), second.astype(np.float32)


def wall_profile(points):
    final_row = points - 1
    j = np.arange(points)
    weight = np.sin(j * (math.pi / final_row)) ** 4
    return np.repeat(weight[:, None], 128, 1).astype(np.float32)


def like(*shape):
    return jax.ShapeDtypeStruct(shape, f32)


def row_profile(at_ref, points, shape):
    row = at_ref[0] * shape[0] + lax.broadcasted_iota(jnp.int32, shape, 0)
    weight = jnp.sin(row.astype(f32) * (math.pi / (points - 1))) ** 4
    wall = jnp.where((row == 0) | (row == points - 1), 1.0, 0.0).astype(f32)
    return weight, wall


def load(pairs, sems):
    copies = [pltpu.make_async_copy(src, dst, sems.at[i]) for i, (src, dst) in enumerate(pairs)]
    for copy in copies:
        copy.start()
    for copy in copies:
        copy.wait()


def z_faces(held, zed_out):
    half = zed_out.shape[0]

    def plane(x, _):
        lane = lax.broadcasted_iota(jnp.int32, zed_out.shape[1:], 1)
        total = jnp.zeros(zed_out.shape[1:], f32)
        for c in range(8):
            for side in range(2):
                at = 8 * c + 64 * side
                moved = pltpu.roll(held[c, x + half * side], 4 + at, 1)
                total = jnp.where((lane >= at) & (lane < at + 8), moved, total)
        zed_out[x] = total
        return 0

    lax.fori_loop(0, half, plane, 0, unroll=2)


def pack_kernel(core_ref, fields_any, cot_any, sent_out, zed_out, last_out, lead_out, held, sems):
    cells = fields_any.shape[1]
    copies = [
        pltpu.make_async_copy(fields_any, held.at[0:4], sems.at[0]),
        pltpu.make_async_copy(cot_any, held.at[4:8], sems.at[1]),
    ]
    for copy in copies:
        copy.start()
    for part, copy in enumerate(copies):
        copy.wait()
        for c in range(4 * part, 4 * part + 4):
            sent_out[:, c] = held[c]
            last_out[c] = held[c, cells - 4 : cells]
            lead_out[c] = held[c, 0:4]

    @pl.when(core_ref[0] % 2 == 1)
    def _():
        z_faces(held, zed_out)


def late_faces_kernel(core_ref, fields_any, cot_any, _lined, zed_out, held, sems):
    @pl.when(core_ref[0] % 2 == 0)
    def _():
        load([(fields_any, held.at[0:4]), (cot_any, held.at[4:8])], sems)
        z_faces(held, zed_out)


def order_kernel(_zed, _last, _lead, _same_last, _same_lead):
    pass


def stencils(values, space, need_first, need_second):
    first = second = None
    if need_first:
        for k in range(4):
            term = (first_coeffs[k] / space) * (values[5 + k] - values[3 - k])
            first = term if first is None else first + term
    if need_second:
        second = (center_coeff / (space * space)) * values[4]
        for k in range(4):
            second = second + (second_coeffs[k] / (space * space)) * (values[5 + k] + values[3 - k])
    return first, second


def along_z_work(
    core, points, core_ref, at_ref, fields_any, prev_any, cot_any, zed_ref,
    res_ref, adj_ref, field_ref, cot_ref, prev_ref, sems,
):
    cells, rows, lanes = fields_any.shape[1:]
    half = cells // 2

    @pl.when(core_ref[0] % 2 == core)
    def _():
        load([(fields_any, field_ref), (cot_any, cot_ref), (prev_any, prev_ref)], sems)
        weight, wall = row_profile(at_ref, points, (rows, lanes))

        def plane(side, step, _):
            x = step + half * side
            lane = lax.broadcasted_iota(jnp.int32, (rows, lanes), 1)
            packed = zed_ref[step]
            u = [field_ref[c, x] for c in range(4)]
            w = [weight * cot_ref[c, x] for c in range(4)]
            far = [pltpu.roll(packed, (lanes - 4 - 8 * c - 64 * side) % lanes, 1) for c in range(8)]
            far_u = far[0:4]
            far_w = [weight * value for value in far[4:8]]

            def along(own, other, need_first, need_second):
                values = [None] * 9
                values[4] = own
                for k in range(1, 5):
                    values[4 + k] = pltpu.roll(jnp.where(lane < k, other, own), lanes - k, 1)
                    values[4 - k] = pltpu.roll(jnp.where(lane >= lanes - k, other, own), k, 1)
                return stencils(values, SPACE_Z, need_first, need_second)

            du = [along(u[c], far_u[c], True, c < 3) for c in range(4)]
            for c in range(3):
                moment = (u[c] - prev_ref[c, x]) * (1.0 / STEP_DT) + u[2] * du[c][0] - NU_VALUE * du[c][1]
                if c == 2:
                    moment = moment + du[3][0]
                res_ref[c, x] = weight * moment + wall * u[c]
            res_ref[3, x] = weight * du[2][0]
            dw = [along(w[c], far_w[c], c >= 2, c < 3) for c in range(4)]
            for c in range(3):
                flux = along(u[2] * w[c], far_u[2] * far_w[c], True, False)[0]
                total = w[c] * (1.0 / STEP_DT) - flux - NU_VALUE * dw[c][1] + wall * cot_ref[c, x]
                if c == 2:
                    stretch = w[0] * du[0][0] + w[1] * du[1][0] + w[2] * du[2][0]
                    total = total + stretch - dw[3][0]
                adj_ref[c, x] = total
            adj_ref[3, x] = -dw[2][0]
            return 0

        for side in range(2):
            lax.fori_loop(0, half, functools.partial(plane, side), 0, unroll=1 + (core == 0))


def early_z_kernel(
    points, core_ref, at_ref, fields_any, prev_any, cot_any, zed_ref, _packed,
    _same, res_ref, adj_ref, *scratch,
):
    along_z_work(
        1, points, core_ref, at_ref, fields_any, prev_any, cot_any, zed_ref, res_ref, adj_ref, *scratch
    )


def late_z_kernel(
    points, core_ref, at_ref, fields_any, prev_any, cot_any, zed_ref, _res, _adj,
    res_ref, adj_ref, *scratch,
):
    along_z_work(
        0, points, core_ref, at_ref, fields_any, prev_any, cot_any, zed_ref, res_ref, adj_ref, *scratch
    )


def along_x_kernel(
    points, at_ref, fields_any, cot_any, before_any, after_any, _res, _adj,
    res_ref, adj_ref, ext, cot_ref, sems,
):
    cells, rows, lanes = fields_any.shape[1:]
    load(
        [
            (fields_any, ext.at[0:4, 4 : 4 + cells]),
            (before_any.at[0:4], ext.at[0:4, 0:4]),
            (after_any.at[0:4], ext.at[0:4, 4 + cells : 8 + cells]),
            (cot_any, cot_ref.at[:, 4 : 4 + cells]),
            (before_any.at[4:8], cot_ref.at[:, 0:4]),
            (after_any.at[4:8], cot_ref.at[:, 4 + cells : 8 + cells]),
        ],
        sems,
    )
    weight = row_profile(at_ref, points, (rows, lanes))[0]

    for c in range(4):
        for x in range(cells + 8):
            value = weight * cot_ref[c, x]
            ext[4 + c, x] = value
            if c < 3:
                ext[8 + c, x] = ext[0, x] * value

    def plane(x, _):
        def along(c, need_first, need_second):
            return stencils([ext[c, x + k] for k in range(9)], SPACE_X, need_first, need_second)

        u = ext[0, 4 + x]
        w = [ext[4 + c, 4 + x] for c in range(3)]
        du = [along(c, True, c < 3) for c in range(4)]
        for c in range(3):
            moment = u * du[c][0] - NU_VALUE * du[c][1]
            if c == 0:
                moment = moment + du[3][0]
            res_ref[c, x] += weight * moment
        res_ref[3, x] += weight * du[0][0]
        dw = [along(4 + c, c in (0, 3), c < 3) for c in range(4)]
        for c in range(3):
            total = -along(8 + c, True, False)[0] - NU_VALUE * dw[c][1]
            if c == 0:
                total = total + (w[0] * du[0][0] + w[1] * du[1][0] + w[2] * du[2][0]) - dw[3][0]
            adj_ref[c, x] += total
        adj_ref[3, x] += -dw[0][0]
        return 0

    lax.fori_loop(0, cells, plane, 0)


def lines(ref, c):
    groups, _, rows, lanes = ref.shape
    return ref[:, c].reshape(groups * rows, lanes)


def blocks(value, groups):
    return value.reshape(groups, value.shape[0] // groups, value.shape[1])


def product(matrix_ref, values):
    lanes = values[0].shape[1]
    wide = jnp.dot(
        matrix_ref[...], jnp.concatenate(values, axis=1), precision=EXACT, preferred_element_type=f32
    )
    return [wide[:, i * lanes : (i + 1) * lanes] for i in range(len(values))]


def lines_kernel(
    first_ref, second_ref, first_t_ref, second_t_ref, weight_ref, in_ref, out_ref, held, sems
):
    groups = in_ref.shape[0]
    weight = weight_ref[...]
    copies = []

    def send(slot, value):
        held[slot] = blocks(value, groups)
        copies.append(pltpu.make_async_copy(held.at[slot], out_ref.at[:, slot], sems.at[slot]))
        copies[-1].start()

    u = [lines(in_ref, c) for c in range(4)]
    w = [weight * lines(in_ref, 4 + c) for c in range(4)]
    slope_2, slope_1 = product(first_ref, [u[1], u[0]])
    press, lifted_1 = product(first_t_ref, [w[1], u[1] * w[0]])
    curve_1, curve_3 = product(second_ref, [u[0], u[2]])
    send(0, weight * (u[1] * slope_1 - NU_VALUE * curve_1))
    send(3, weight * slope_2)
    send(7, press)
    slope_3, joint = product(first_ref, [u[2], u[3] - NU_VALUE * slope_2])
    send(1, weight * (u[1] * slope_2 + joint))
    send(2, weight * (u[1] * slope_3 - NU_VALUE * curve_3))
    stretch = w[0] * slope_1 + w[1] * slope_2 + w[2] * slope_3
    bent_1, bent_3 = product(second_t_ref, [w[0], w[2]])
    send(4, lifted_1 - NU_VALUE * bent_1)
    lifted_2, lifted_3 = product(first_t_ref, [u[1] * w[1] + w[3] - NU_VALUE * press, u[1] * w[2]])
    send(5, lifted_2 + stretch)
    send(6, lifted_3 - NU_VALUE * bent_3)
    for copy in copies:
        copy.wait()


def add_kernel(res_ref, adj_ref, back_ref, res_out, adj_out, held, sems):
    copies = []
    for c in range(8):
        part, out = (res_ref, res_out) if c < 4 else (adj_ref, adj_out)
        held[c] = part[c % 4] + back_ref[:, c]
        copies.append(pltpu.make_async_copy(held.at[c], out.at[c % 4], sems.at[c]))
        copies[-1].start()
    for copy in copies:
        copy.wait()


def per_device(fields, previous, cotangent):
    cells, rows, lanes = fields.shape[1:]
    groups = lax.axis_size("gy")
    points = rows * groups
    first, second = wall_matrices(points)
    weight = wall_profile(points)
    sent = (cells, 8, rows, lanes)
    gx, gz = lax.axis_size("gx"), lax.axis_size("gz")
    at = lax.axis_index("gy").astype(jnp.int32).reshape(1)
    core_at = lax.axis_index("gx").astype(jnp.int32).reshape(1)
    exchange = functools.partial(lax.all_to_all, axis_name="gy", split_axis=0, concat_axis=0, tiled=True)
    far = pl.BlockSpec(memory_space=pltpu.HBM)
    near = pl.BlockSpec(memory_space=pltpu.VMEM)
    any_place = pl.BlockSpec(memory_space=pl.ANY)
    scalars = pl.BlockSpec(memory_space=pltpu.SMEM)
    plane = (rows, lanes)
    limit = pltpu.CompilerParams(vmem_limit_bytes=WIDE_BYTES)

    zed_shape = pltpu.VMEM((cells // 2,) + plane, f32)
    face = pltpu.VMEM((8, 4) + plane, f32)

    def swap_zed(zed, core):
        pairs = [(x * gz + z, x * gz + (z + 1) % gz) for x in range(core, gx, 2) for z in range(gz)]
        return pltpu.with_memory_space_constraint(lax.ppermute(zed, ("gx", "gz"), pairs), pltpu.VMEM)

    packed, zed, last, lead = pl.pallas_call(
        pack_kernel,
        out_shape=[pltpu.VMEM(sent, f32), zed_shape, face, face],
        in_specs=[scalars, far, far],
        out_specs=[near] * 4,
        scratch_shapes=[pltpu.VMEM((8, cells) + plane, f32), pltpu.SemaphoreType.DMA((2,))],
        compiler_params=limit,
    )(core_at, fields, cotangent)

    z_scratch = [
        pltpu.VMEM((4, cells) + plane, f32),
        pltpu.VMEM((4, cells) + plane, f32),
        pltpu.VMEM((3, cells) + plane, f32),
        pltpu.SemaphoreType.DMA((3,)),
    ]
    part = pltpu.VMEM((4, cells) + plane, f32)
    cost = pl.CostEstimate(flops=2 * 10**7, bytes_accessed=6 * 10**6, transcendentals=0)

    packed, res, adj = pl.pallas_call(
        functools.partial(early_z_kernel, points),
        out_shape=[pltpu.VMEM(sent, f32), part, part],
        in_specs=[scalars] * 2 + [far] * 3 + [near] * 2,
        out_specs=[near] * 3,
        scratch_shapes=z_scratch,
        input_output_aliases={6: 0},
        cost_estimate=cost,
        compiler_params=limit,
    )(core_at, at, fields, previous, cotangent, swap_zed(zed, 1), packed)
    gathered = exchange(packed)

    matrices = [first, second, np.ascontiguousarray(first.T), np.ascontiguousarray(second.T), weight]
    resident = pl.BlockSpec(memory_space=pltpu.VMEM)
    lined = pl.pallas_call(
        lines_kernel,
        out_shape=like(groups, 8, rows, lanes),
        in_specs=[resident] * 6,
        out_specs=far,
        scratch_shapes=[pltpu.VMEM((8, groups, rows, lanes), f32), pltpu.SemaphoreType.DMA((8,))],
        cost_estimate=pl.CostEstimate(
            flops=2 * points * points * lanes * 14 * 6, bytes_accessed=4 * 10**6, transcendentals=0
        ),
        compiler_params=pltpu.CompilerParams(vmem_limit_bytes=VMEM_BYTES),
    )(*[jnp.asarray(m) for m in matrices], gathered)

    zed_later = pl.pallas_call(
        late_faces_kernel,
        out_shape=zed_shape,
        in_specs=[scalars] + [far] * 3,
        scratch_shapes=[pltpu.VMEM((8, cells) + plane, f32), pltpu.SemaphoreType.DMA((2,))],
        cost_estimate=cost,
        compiler_params=limit,
    )(core_at, fields, cotangent, lined)
    even_zed = swap_zed(zed_later, 0)
    last, lead = pl.pallas_call(
        order_kernel,
        out_shape=[face, face],
        in_specs=[near] * 3,
        input_output_aliases={1: 0, 2: 1},
        compiler_params=limit,
    )(even_zed, last, lead)
    res, adj = pl.pallas_call(
        functools.partial(late_z_kernel, points),
        out_shape=[part, part],
        in_specs=[scalars] * 2 + [far] * 3 + [near] * 3,
        scratch_shapes=z_scratch,
        input_output_aliases={6: 0, 7: 1},
        cost_estimate=cost,
        compiler_params=limit,
    )(core_at, at, fields, previous, cotangent, even_zed, res, adj)

    before = lax.ppermute(last, "gx", [(i, (i + 1) % gx) for i in range(gx)])
    after = lax.ppermute(lead, "gx", [((i + 1) % gx, i) for i in range(gx)])
    res, adj = pl.pallas_call(
        functools.partial(along_x_kernel, points),
        out_shape=[part, part],
        in_specs=[scalars] + [far] * 2 + [near] * 4,
        scratch_shapes=[
            pltpu.VMEM((11, cells + 8) + plane, f32),
            pltpu.VMEM((4, cells + 8) + plane, f32),
            pltpu.SemaphoreType.DMA((6,)),
        ],
        input_output_aliases={5: 0, 6: 1},
        cost_estimate=cost,
        compiler_params=limit,
    )(at, fields, cotangent, *(pltpu.with_memory_space_constraint(v, pltpu.VMEM) for v in (before, after)), res, adj)

    back = exchange(lined)
    block = like(4, cells, rows, lanes)
    residual, adjoint = pl.pallas_call(
        add_kernel,
        out_shape=[block, block],
        in_specs=[near] * 3,
        out_specs=[far] * 2,
        scratch_shapes=[pltpu.VMEM((8, cells) + plane, f32), pltpu.SemaphoreType.DMA((8,))],
        compiler_params=pltpu.CompilerParams(vmem_limit_bytes=VMEM_BYTES),
    )(res, adj, back)
    return residual, adjoint


def solution(mesh):
    spec = P(None, "gx", "gy", "gz")
    return jax.shard_map(
        per_device, mesh=mesh, in_specs=(spec,) * 3, out_specs=(spec,) * 2, check_vma=False
    )
```
